32 devices in a mesh: seq: 4 (over z), head: 8 (over y, x, core).
Axes of the slice: x: 2, y: 2, z: 4, core: 2. Of those that a mesh axis runs over, the one named last changes fastest.
Arguments:
- queries: bfloat16 [4096, 8192], P('seq', 'head'), may hold values from -6 to 6
- keys: bfloat16 [4096, 8192], P('seq', 'head'), may hold values from -1 to 1
- values: bfloat16 [4096, 8192], P('seq', 'head'), may hold values from -40 to 40
- log_decay: float32 [64, 4096], P('head', 'seq'), may hold values from -1 to 0
- gain: float32 [8192], P('head'), may hold values from 0.25 to 1.75
- out_grad: bfloat16 [4096, 8192], P('seq', 'head'), may hold values from -16 to 16
Outputs:
- output: bfloat16 [4096, 8192], P('seq', 'head')
- query_grad: bfloat16 [4096, 8192], P('seq', 'head')
- key_grad: bfloat16 [4096, 8192], P('seq', 'head')
- value_grad: bfloat16 [4096, 8192], P('seq', 'head')
- gain_grad: float32 [8192], P('head')
The draws below stay inside these ranges and needn't reach their ends.
All inputs are finite; a program needn't handle non-finite values.
Results may differ from the reference program's by a relative error of at most 0.001.
Values sent between devices are 32-bit elements; how exact they have to be, the bound alone decides.
A program may use at most 128 MiB of HBM per device.

```python
import math
import jax
import jax.numpy as jnp
from jax import lax

HEAD_TOTAL = 64
HEAD_DIM = 128
TOK_DEV = 1024
LENGTH = 4096


def head_rates(key):
    rate_key = jax.random.fold_in(key, 7001)
    pick_key, fast_key, slow_key = jax.random.split(rate_key, 3)
    fast_share = 0.5
    is_fast = jax.random.uniform(pick_key, (HEAD_TOTAL,)) < fast_share
    fast_low = math.log(max(1.0 / 50.0, 3.0 / TOK_DEV))
    fast_high = math.log(max(1.0 / 30.0, 4.0 / TOK_DEV))
    fast = jnp.exp(jax.random.uniform(fast_key, (HEAD_TOTAL,), minval=fast_low, maxval=fast_high))
    slow = jnp.exp(jax.random.uniform(slow_key, (HEAD_TOTAL,), minval=math.log(0.05 / LENGTH), maxval=math.log(0.6 / LENGTH)))
    return jnp.where(is_fast, fast, slow)


def draw_log_decay(key, part):
    rates = head_rates(key)
    spike_seed_key = jax.random.fold_in(key, 7002)
    position_seed_key, layer_depth_key = jax.random.split(spike_seed_key)
    token_places = jax.random.randint(position_seed_key, (HEAD_TOTAL, 2), 0, LENGTH)
    spike_log_values = jnp.log(jax.random.uniform(layer_depth_key, (HEAD_TOTAL, 2), minval=0.5, maxval=0.8))
    token_positions = jnp.arange(LENGTH)[None, :]
    first_operand = jnp.where(token_positions == token_places[:, 0:1], spike_log_values[:, 0:1], 0.0)
    second_operand = jnp.where(token_positions == token_places[:, 1:2], spike_log_values[:, 1:2], 0.0)
    return (jnp.minimum(first_operand, second_operand) - rates[:, None]).astype(jnp.float32)


def draw_keys(key, part):
    rates = head_rates(key)
    scale = jnp.minimum(1.0, jnp.sqrt(40.0 * rates)) / math.sqrt(HEAD_DIM)
    base_key = jax.random.fold_in(key, 7003)
    base = jnp.clip(jax.random.normal(base_key, (LENGTH, HEAD_TOTAL, HEAD_DIM)), -3.0, 3.0)
    return (base * scale[None, :, None]).reshape(LENGTH, HEAD_TOTAL * HEAD_DIM).astype(jnp.bfloat16)


def draw_values(key, part):
    jitter_key, row_key, base_key = jax.random.split(jax.random.fold_in(key, 7004), 3)
    head_scale = 10.0 ** (jnp.arange(HEAD_TOTAL, dtype=jnp.float32) / (HEAD_TOTAL - 1))
    head_scale = head_scale * jnp.exp(jax.random.uniform(jitter_key, (HEAD_TOTAL,), minval=math.log(0.8), maxval=math.log(1.25)))
    base = jnp.clip(jax.random.normal(base_key, (LENGTH, HEAD_TOTAL, HEAD_DIM)), -3.0, 3.0)
    row_scale = jnp.exp(jax.random.uniform(row_key, (LENGTH,), minval=0.0, maxval=math.log(10.0)))
    result = base * head_scale[None, :, None] * row_scale[:, None, None] / 10.0
    return result.reshape(LENGTH, HEAD_TOTAL * HEAD_DIM).astype(jnp.bfloat16)


def draw_out_grad(key, part):
    base_key = jax.random.fold_in(jax.random.fold_in(key, 7005), 0)
    jitter_key = jax.random.fold_in(jax.random.fold_in(key, 7005), 2)
    along = jnp.arange(LENGTH, dtype=jnp.float32) / (LENGTH - 1)
    jitter = jnp.exp(jax.random.uniform(jitter_key, (LENGTH,), minval=math.log(0.7), maxval=math.log(1.4)))
    base = jnp.clip(jax.random.normal(base_key, (LENGTH, HEAD_TOTAL * HEAD_DIM)), -3.0, 3.0)
    rising = 0.5 * 3.0 ** along
    return (base * (rising * jitter)[:, None]).astype(jnp.bfloat16)


def block_scale(own_key, dims, cuts, low, largest):
    loudness, own = 1.0, jax.random.fold_in(own_key, 6)
    for dim, shards_of in cuts:
        heights = jnp.exp(jax.random.uniform(jax.random.fold_in(own, dim), (shards_of,), jnp.float32, low / len(cuts), largest / len(cuts)))
        loudness = loudness * jnp.repeat(heights, dims[dim] // shards_of).reshape([-1 if axis == dim else 1 for axis in range(len(dims))])
    return loudness


def scatter_about(stream_key, shape, width, most, shards=(), kind=jnp.bfloat16):
    values = width * jax.random.normal(stream_key, shape, jnp.float32)
    if shards:
        values = values * block_scale(stream_key, shape, shards, -0.22, 0.18)
    return jnp.clip(values, -most, most).astype(kind)


def setup_inputs(seed: int = 0) -> dict:
    arg_keys = jax.random.split(jax.random.key(seed), 7)
    queries = scatter_about(arg_keys[0], (LENGTH, HEAD_TOTAL * HEAD_DIM), 1.0, 6.0, ((0, 4), (1, 8)))
    keys = draw_keys(jax.random.fold_in(arg_keys[6], 71), 0)
    values = draw_values(jax.random.fold_in(arg_keys[6], 71), 0)
    log_decay = draw_log_decay(jax.random.fold_in(arg_keys[6], 71), 0)
    gain = jnp.clip(1.0 + 0.15 * jax.random.normal(arg_keys[4], (HEAD_TOTAL * HEAD_DIM,), jnp.float32), 0.25, 1.75)
    out_grad = draw_out_grad(jax.random.fold_in(arg_keys[6], 71), 0)
    return {"queries": queries, "keys": keys, "values": values, "log_decay": log_decay, "gain": gain, "out_grad": out_grad}


epsilon = 1e-06
highest = lax.Precision.HIGHEST

def attention(query_heads, key_heads, value_heads, log_decay):
    head_count, length, head_width = query_heads.shape
    block_rows = min(256, length)
    block_count = length // block_rows

    def blocks(matrix):
        return matrix.reshape(head_count, block_count, block_rows, head_width).transpose(1, 0, 2, 3)
    decay_blocks = log_decay.reshape(head_count, block_count, block_rows).transpose(1, 0, 2)
    causal = jnp.arange(block_rows)[:, None] >= jnp.arange(block_rows)[None, :]

    def block_step(carry_state, inputs):
        query_block, key_block, value_block, decay_block = inputs
        decay_sum = jnp.cumsum(decay_block, axis=1)
        block_total = decay_sum[:, -1]
        mask_decay = jnp.exp(jnp.where(causal, decay_sum[:, :, None] - decay_sum[:, None, :], -1e+30))
        scores = jnp.einsum('hid,hjd->hij', query_block, key_block, precision=highest) * mask_decay
        inside = jnp.einsum('hij,hjd->hid', scores, value_block, precision=highest)
        carried = jnp.exp(decay_sum)[:, :, None] * jnp.einsum('hid,hde->hie', query_block, carry_state, precision=highest)
        weighted = key_block * jnp.exp(block_total[:, None] - decay_sum)[:, :, None]
        carry_state = jnp.exp(block_total)[:, None, None] * carry_state + jnp.einsum('hjd,hje->hde', weighted, value_block, precision=highest)
        return (carry_state, inside + carried)
    initial = jnp.zeros((head_count, head_width, head_width), jnp.float32)
    _, result = lax.scan(jax.checkpoint(block_step), initial, (blocks(query_heads), blocks(key_heads), blocks(value_heads), decay_blocks))
    return result.transpose(1, 0, 2, 3).reshape(head_count, length, head_width)

def reference(queries, keys, values, log_decay, gain, out_grad):
    length, channels = queries.shape

    def to_heads(matrix):
        return matrix.astype(jnp.float32).reshape(length, HEAD_TOTAL, HEAD_DIM).transpose(1, 0, 2)

    def from_heads(heads_array):
        return heads_array.transpose(1, 0, 2).reshape(length, channels).astype(jnp.bfloat16)

    def forward(query_heads, key_heads, value_heads, gain_vector):
        attended = attention(query_heads, key_heads, value_heads, log_decay)
        flattened = attended.transpose(1, 0, 2).reshape(length, channels)
        root_mean = jnp.sqrt(lax.optimization_barrier(jnp.mean(flattened * flattened, axis=1, keepdims=True)) + epsilon)
        return flattened / root_mean * gain_vector
    output, pullback = jax.vjp(forward, to_heads(queries), to_heads(keys), to_heads(values), gain)
    query_grad, key_grad, value_grad, gain_grad = pullback(out_grad.astype(jnp.float32))
    return (output.astype(jnp.bfloat16), from_heads(query_grad), from_heads(key_grad), from_heads(value_grad), gain_grad)
```

```python
import functools

import jax
import jax.numpy as jnp
from jax import lax
from jax.experimental import pallas as pl
from jax.experimental.pallas import tpu as pltpu
from jax.sharding import PartitionSpec as P

epsilon = 1e-06
highest = lax.Precision.HIGHEST
MESH = pl.DeviceIdType.MESH
WIDTH = 128
f32, bf16 = jnp.float32, jnp.bfloat16


def dot(a, b, ca=1, cb=0):
    return lax.dot_general(a, b, (((ca,), (cb,)), ((), ())), preferred_element_type=f32)


def split(x):
    high = x.astype(bf16)
    return high, (x - high.astype(f32)).astype(bf16)


def kernel(
    seq_count, head_count, heads, rows,
    decay, gain, q_hbm, k_hbm, v_hbm, g_hbm,
    out_hbm, dq_hbm, dk_hbm, dv_hbm, dgain,
    q, k, v, g, out, dq, dk, dv,
    attn, sums_g, cols_g, own, entering, back, mask, p_high, p_low,
    f_in, f_out, b_in, b_out, acc_sq, acc_pr, norm, alpha, beta, gparts,
    in_sem, out_sem, f_send, f_recv, b_send, b_recv, n_send, n_recv, g_send, g_recv,
):
    z = lax.axis_index("seq")
    me = lax.axis_index("head")
    size = min(256, rows)
    count = rows // size
    channels = heads * WIDTH * head_count

    def cols(h):
        return pl.ds(pl.multiple_of(h * WIDTH, WIDTH), WIDTH)

    def load(n, h):
        hbm, ref = ((k_hbm, k), (v_hbm, v), (q_hbm, q), (g_hbm, g))[n]
        return pltpu.make_async_copy(hbm.at[:, cols(h)], ref.at[:, cols(h)], in_sem.at[n, h])

    def store(n, h):
        hbm, ref = ((out_hbm, out), (dq_hbm, dq), (dk_hbm, dk), (dv_hbm, dv))[n]
        return pltpu.make_async_copy(ref.at[:, cols(h)], hbm.at[:, cols(h)], out_sem.at[n, h])

    def forward(h):
        return pltpu.make_async_remote_copy(
            src_ref=f_out.at[h], dst_ref=f_in.at[h], send_sem=f_send.at[h], recv_sem=f_recv.at[h],
            device_id=(lax.rem(z + 1, seq_count), me), device_id_type=MESH)

    def backward(h):
        return pltpu.make_async_remote_copy(
            src_ref=b_out.at[h], dst_ref=b_in.at[h], send_sem=b_send.at[h], recv_sem=b_recv.at[h],
            device_id=(lax.rem(z + seq_count - 1, seq_count), me), device_id_type=MESH)

    for h in range(heads):
        load(0, h).start()
        load(1, h).start()
    for h in range(heads):
        load(2, h).start()
        load(3, h).start()

    barrier = pltpu.get_barrier_semaphore()
    for step in range(1, head_count):
        pl.semaphore_signal(barrier, inc=1, device_id=(z, lax.rem(me + step, head_count)), device_id_type=MESH)
    for step in range(1, seq_count):
        pl.semaphore_signal(barrier, inc=1, device_id=(lax.rem(z + step, seq_count), me), device_id_type=MESH)

    below = lax.broadcasted_iota(jnp.int32, (size, size), 0) >= lax.broadcasted_iota(jnp.int32, (size, size), 1)
    above = lax.broadcasted_iota(jnp.int32, (size, size), 0) <= lax.broadcasted_iota(jnp.int32, (size, size), 1)
    tri = jnp.where(above, 1.0, 0.0).astype(f32)
    for b in range(count):
        at = pl.ds(b * size, size)
        sums_g[:, at] = jnp.dot(decay[:, at], tri, precision=highest, preferred_element_type=f32)
    acc_sq[...] = jnp.zeros_like(acc_sq)
    acc_pr[...] = jnp.zeros_like(acc_pr)
    pl.semaphore_wait(barrier, head_count - 1 + seq_count - 1)

    def total(h, b):
        return cols_g[(b + 1) * size - 1:(b + 1) * size, cols(h)]

    def states(h, carry):
        load(0, h).wait()
        load(1, h).wait()
        state = jnp.zeros((WIDTH, WIDTH), f32)
        for b in range(count):
            at = pl.ds(b * size, size)
            column = jnp.broadcast_to(sums_g[pl.ds(h, 1), at], (WIDTH, size)).T
            cols_g[at, cols(h)] = column
            last = column[size - 1:size, :]
            high, low = split(v[at, cols(h)].astype(f32) * jnp.exp(last - column))
            both = dot(k[at, cols(h)], jnp.concatenate([high, low], axis=1), 0, 0)
            mine = both[:, :WIDTH] + both[:, WIDTH:]
            own[h, b] = mine
            state = jnp.exp(last) * state + mine
        f_out[h] = state

        @pl.when(z == 0)
        def _():
            f_in[h] = jnp.zeros((WIDTH, WIDTH), f32)
            forward(h).start()
        return carry

    lax.fori_loop(0, heads, states, 0)

    def device_total(h):
        result = total(h, 0)
        for b in range(1, count):
            result = result + total(h, b)
        return result

    def attend(h, carry):
        load(2, h).wait()
        load(3, h).wait()
        for b in range(count):
            at = pl.ds(b * size, size)
            wide = jnp.concatenate([cols_g[at, cols(h)]] * (size // WIDTH), axis=1)
            m = jnp.exp(jnp.where(below, wide - sums_g[pl.ds(h, 1), at], -1e30))
            mask[h, at, :] = m
            high, low = split(dot(q[at, cols(h)], k[at, cols(h)], 1, 1) * m)
            p_high[h, at, :] = high
            p_low[h, at, :] = low
            attn[at, cols(h)] = dot(high, v[at, cols(h)]) + dot(low, v[at, cols(h)])

        @pl.when(z > 0)
        def _():
            forward(h).wait_recv()

            @pl.when(z < seq_count - 1)
            def _():
                f_out[h] = f_out[h] + jnp.exp(device_total(h)) * f_in[h]
                forward(h).start()

        state = f_in[h]
        for b in range(count):
            at = pl.ds(b * size, size)
            entering[h, b] = state
            high, low = split(state)
            query = q[at, cols(h)]
            cross = dot(jnp.concatenate([query, query], axis=1), jnp.concatenate([high, low], axis=0))
            value = attn[at, cols(h)] + jnp.exp(cols_g[at, cols(h)]) * cross
            attn[at, cols(h)] = value
            acc_sq[at, :] = acc_sq[at, :] + value * value
            acc_pr[at, :] = acc_pr[at, :] + value * (g[at, cols(h)].astype(f32) * gain[:, cols(h)])
            state = jnp.exp(total(h, b)) * state + own[h, b]
        return carry

    lax.fori_loop(0, heads, attend, 0)

    for b in range(rows // WIDTH):
        at = pl.ds(b * WIDTH, WIDTH)
        norm[me, 0:1, at] = jnp.sum(acc_sq[at, :].T, axis=0, keepdims=True)
        norm[me, 1:2, at] = jnp.sum(acc_pr[at, :].T, axis=0, keepdims=True)

    def exchange(step):
        return pltpu.make_async_remote_copy(
            src_ref=norm.at[me], dst_ref=norm.at[me], send_sem=n_send.at[step], recv_sem=n_recv.at[step],
            device_id=(z, lax.rem(me + step, head_count)), device_id_type=MESH)

    def arrived(step):
        slot = norm.at[lax.rem(me + head_count - step, head_count)]
        return pltpu.make_async_remote_copy(
            src_ref=slot, dst_ref=slot, send_sem=n_send.at[step], recv_sem=n_recv.at[step],
            device_id=(z, lax.rem(me + step, head_count)), device_id_type=MESH)

    for step in range(1, head_count):
        exchange(step).start()
    for step in range(1, head_count):
        arrived(step).wait_recv()
    summed = norm[0]
    for d in range(1, head_count):
        summed = summed + norm[d]
    inverse = 1.0 / jnp.sqrt(summed[0:1] / channels + epsilon)
    second = inverse * inverse * inverse * (summed[1:2] / channels)
    for b in range(rows // WIDTH):
        at = slice(b * WIDTH, (b + 1) * WIDTH)
        alpha[at, :] = jnp.broadcast_to(inverse[:, at], (WIDTH, WIDTH)).T
        beta[at, :] = jnp.broadcast_to(second[:, at], (WIDTH, WIDTH)).T

    def gradients(h, carry):
        gain_h = gain[:, cols(h)]
        part = jnp.zeros((1, WIDTH), f32)
        state = jnp.zeros((WIDTH, WIDTH), f32)
        for b in reversed(range(count)):
            at = pl.ds(b * size, size)
            scale = alpha[at, :]
            value = attn[at, cols(h)]
            cotangent = g[at, cols(h)].astype(f32)
            normed = value * scale
            out[at, cols(h)] = (normed * gain_h).astype(bf16)
            part = part + jnp.sum(cotangent * normed, axis=0, keepdims=True)
            a = scale * (cotangent * gain_h) - beta[at, :] * value
            attn[at, cols(h)] = a
            high, low = split(a * jnp.exp(cols_g[at, cols(h)]))
            both = dot(q[at, cols(h)], jnp.concatenate([high, low], axis=1), 0, 0)
            mine = both[:, :WIDTH] + both[:, WIDTH:]
            back[h, b] = mine
            state = jnp.exp(total(h, b)) * state + mine
        gparts[z, :, cols(h)] = part
        b_out[h] = state
        store(0, h).start()

        @pl.when(z == seq_count - 1)
        def _():
            b_in[h] = jnp.zeros((WIDTH, WIDTH), f32)
            backward(h).start()
        return carry

    lax.fori_loop(0, heads, gradients, 0)

    def gain_copy(step, slot):
        return pltpu.make_async_remote_copy(
            src_ref=gparts.at[slot], dst_ref=gparts.at[slot], send_sem=g_send.at[step], recv_sem=g_recv.at[step],
            device_id=(lax.rem(z + step, seq_count), me), device_id_type=MESH)

    for step in range(1, seq_count):
        gain_copy(step, z).start()

    def finish(h, carry):
        @pl.when(z < seq_count - 1)
        def _():
            backward(h).wait_recv()

            @pl.when(z > 0)
            def _():
                b_out[h] = b_out[h] + jnp.exp(device_total(h)) * b_in[h]
                backward(h).start()

        state = b_in[h]
        for b in reversed(range(count)):
            at = pl.ds(b * size, size)
            query, key, value = q[at, cols(h)], k[at, cols(h)], v[at, cols(h)]
            a_high, a_low = split(attn[at, cols(h)])
            a_both = jnp.concatenate([a_high, a_low], axis=1)
            ds = dot(a_both, jnp.concatenate([value, value], axis=1), 1, 1) * mask[h, at, :]
            ds_high, ds_low = split(ds)
            column = cols_g[at, cols(h)]
            e_high, e_low = split(entering[h, b])
            cross = dot(a_both, jnp.concatenate([e_high, e_high], axis=1), 1, 1) + dot(a_high, e_low, 1, 1)
            dq[at, cols(h)] = (
                dot(ds_high, key) + dot(ds_low, key) + jnp.exp(column) * cross
            ).astype(bf16)
            to_end = jnp.exp(total(h, b) - column)
            s_high, s_low = split(state)
            from_later = dot(jnp.concatenate([value, value], axis=1), jnp.concatenate([s_high, s_low], axis=1), 1, 1)
            dk[at, cols(h)] = (
                dot(ds_high, query, 0, 0) + dot(ds_low, query, 0, 0) + to_end * from_later
            ).astype(bf16)
            from_later = dot(jnp.concatenate([key, key], axis=1), jnp.concatenate([s_high, s_low], axis=0))
            both = dot(p_high[h, at, :], a_both, 0, 0)
            dv[at, cols(h)] = (
                both[:, :WIDTH] + both[:, WIDTH:] + dot(p_low[h, at, :], a_high, 0, 0) + to_end * from_later
            ).astype(bf16)
            state = jnp.exp(total(h, b)) * state + back[h, b]
        store(1, h).start()
        store(2, h).start()
        store(3, h).start()
        return carry

    lax.fori_loop(0, heads, finish, 0)

    for step in range(1, seq_count):
        gain_copy(step, lax.rem(z + seq_count - step, seq_count)).wait_recv()
    result = gparts[0]
    for d in range(1, seq_count):
        result = result + gparts[d]
    dgain[...] = result

    for step in range(1, seq_count):
        gain_copy(step, z).wait_send()
    for step in range(1, head_count):
        exchange(step).wait_send()
    for h in range(heads):
        for n in range(4):
            store(n, h).wait()

    @pl.when(z < seq_count - 1)
    def _():
        for h in range(heads):
            forward(h).wait_send()

    @pl.when(z > 0)
    def _():
        for h in range(heads):
            backward(h).wait_send()


def local(queries, keys, values, log_decay, gain, out_grad):
    rows, channels = queries.shape
    heads = log_decay.shape[0]
    seq_count, head_count = lax.axis_size("seq"), lax.axis_size("head")
    size = min(256, rows)
    count = rows // size
    any_spec = pl.BlockSpec(memory_space=pl.ANY)
    vmem_spec = pl.BlockSpec(memory_space=pltpu.VMEM)
    narrow = jax.ShapeDtypeStruct((rows, channels), bf16)
    state = pltpu.VMEM((heads, WIDTH, WIDTH), f32)
    block_states = pltpu.VMEM((heads, count, WIDTH, WIDTH), f32)
    dma = pltpu.SemaphoreType.DMA
    results = pl.pallas_call(
        functools.partial(kernel, seq_count, head_count, heads, rows),
        out_shape=(narrow,) * 4 + (jax.ShapeDtypeStruct((1, channels), f32),),
        in_specs=[vmem_spec, vmem_spec] + [any_spec] * 4,
        out_specs=(any_spec,) * 4 + (vmem_spec,),
        scratch_shapes=[pltpu.VMEM((rows, channels), bf16)] * 8
        + [
            pltpu.VMEM((rows, channels), f32),
            pltpu.VMEM((heads, rows), f32),
            pltpu.VMEM((rows, channels), f32),
            block_states, block_states, block_states,
            pltpu.VMEM((heads, rows, size), f32),
            pltpu.VMEM((heads, rows, size), bf16),
            pltpu.VMEM((heads, rows, size), bf16),
            state, state, state, state,
            pltpu.VMEM((rows, WIDTH), f32),
            pltpu.VMEM((rows, WIDTH), f32),
            pltpu.VMEM((head_count, 2, rows), f32),
            pltpu.VMEM((rows, WIDTH), f32),
            pltpu.VMEM((rows, WIDTH), f32),
            pltpu.VMEM((seq_count, 1, channels), f32),
            dma((4, heads)), dma((4, heads)),
            dma((heads,)), dma((heads,)), dma((heads,)), dma((heads,)),
            dma((head_count,)), dma((head_count,)), dma((seq_count,)), dma((seq_count,)),
        ],
        compiler_params=pltpu.CompilerParams(
            collective_id=0, has_side_effects=True, vmem_limit_bytes=60 * 1024 * 1024
        ),
        name="lightning",
    )(log_decay, gain.reshape(1, channels), queries, keys, values, out_grad)
    return results[:4] + (results[4].reshape(channels),)


def solution(mesh):
    in_specs = (
        P("seq", "head"),
        P("seq", "head"),
        P("seq", "head"),
        P("head", "seq"),
        P("head"),
        P("seq", "head"),
    )
    out_specs = (P("seq", "head"), P("seq", "head"), P("seq", "head"), P("seq", "head"), P("head"))
    return jax.shard_map(local, mesh=mesh, in_specs=in_specs, out_specs=out_specs, check_vma=False)
```

```python
import functools

import jax
import jax.numpy as jnp
from jax import lax
from jax.experimental import pallas as pl
from jax.experimental.pallas import tpu as pltpu
from jax.sharding import PartitionSpec as P

epsilon = 1e-06
highest = lax.Precision.HIGHEST
MESH = pl.DeviceIdType.MESH
WIDTH = 128
f32, bf16 = jnp.float32, jnp.bfloat16


def dot(a, b, ca=1, cb=0):
    return lax.dot_general(a, b, (((ca,), (cb,)), ((), ())), preferred_element_type=f32)


def split(x):
    high = x.astype(bf16)
    return high, (x - high.astype(f32)).astype(bf16)


def kernel(
    seq_count, head_count, heads, rows,
    decay, gain, q_hbm, k_hbm, v_hbm, g_hbm,
    out_hbm, dq_hbm, dk_hbm, dv_hbm, dgain,
    q, k, v, g, out, dq, dk, dv,
    attn, sums_g, cols_g, own, entering, back, mask, p_high, p_low,
    f_in, f_out, b_in, b_out, acc_sq, acc_pr, norm, alpha, beta, gparts,
    in_sem, out_sem, f_send, f_recv, b_send, b_recv, n_send, n_recv, g_send, g_recv,
):
    z = lax.axis_index("seq")
    me = lax.axis_index("head")
    size = min(256, rows)
    count = rows // size
    channels = heads * WIDTH * head_count

    def cols(h):
        return pl.ds(pl.multiple_of(h * WIDTH, WIDTH), WIDTH)

    def load(n, h):
        hbm, ref = ((k_hbm, k), (v_hbm, v), (q_hbm, q), (g_hbm, g))[n]
        return pltpu.make_async_copy(hbm.at[:, cols(h)], ref.at[:, cols(h)], in_sem.at[n, h])

    def store(n, h):
        hbm, ref = ((out_hbm, out), (dq_hbm, dq), (dk_hbm, dk), (dv_hbm, dv))[n]
        return pltpu.make_async_copy(ref.at[:, cols(h)], hbm.at[:, cols(h)], out_sem.at[n, h])

    def forward(h):
        return pltpu.make_async_remote_copy(
            src_ref=f_out.at[h], dst_ref=f_in.at[h], send_sem=f_send.at[h], recv_sem=f_recv.at[h],
            device_id=(lax.rem(z + 1, seq_count), me), device_id_type=MESH)

    def backward(h):
        return pltpu.make_async_remote_copy(
            src_ref=b_out.at[h], dst_ref=b_in.at[h], send_sem=b_send.at[h], recv_sem=b_recv.at[h],
            device_id=(lax.rem(z + seq_count - 1, seq_count), me), device_id_type=MESH)

    for h in range(heads):
        load(0, h).start()
        load(1, h).start()
    for h in range(heads):
        load(2, h).start()
        load(3, h).start()

    barrier = pltpu.get_barrier_semaphore()
    for step in range(1, head_count):
        pl.semaphore_signal(barrier, inc=1, device_id=(z, lax.rem(me + step, head_count)), device_id_type=MESH)
    for step in range(1, seq_count):
        pl.semaphore_signal(barrier, inc=1, device_id=(lax.rem(z + step, seq_count), me), device_id_type=MESH)

    below = lax.broadcasted_iota(jnp.int32, (size, size), 0) >= lax.broadcasted_iota(jnp.int32, (size, size), 1)
    above = lax.broadcasted_iota(jnp.int32, (size, size), 0) <= lax.broadcasted_iota(jnp.int32, (size, size), 1)
    tri = jnp.where(above, 1.0, 0.0).astype(f32)
    for b in range(count):
        at = pl.ds(b * size, size)
        sums_g[:, at] = jnp.dot(decay[:, at], tri, precision=highest, preferred_element_type=f32)
    acc_sq[...] = jnp.zeros_like(acc_sq)
    acc_pr[...] = jnp.zeros_like(acc_pr)
    pl.semaphore_wait(barrier, head_count - 1 + seq_count - 1)

    def total(h, b):
        return cols_g[(b + 1) * size - 1:(b + 1) * size, cols(h)]

    def states(h, carry):
        load(0, h).wait()
        load(1, h).wait()
        state = jnp.zeros((WIDTH, WIDTH), f32)
        for b in range(count):
            at = pl.ds(b * size, size)
            column = jnp.broadcast_to(sums_g[pl.ds(h, 1), at], (WIDTH, size)).T
            cols_g[at, cols(h)] = column
            last = column[size - 1:size, :]
            high, low = split(v[at, cols(h)].astype(f32) * jnp.exp(last - column))
            both = dot(k[at, cols(h)], jnp.concatenate([high, low], axis=1), 0, 0)
            mine = both[:, :WIDTH] + both[:, WIDTH:]
            own[h, b] = mine
            state = jnp.exp(last) * state + mine
        f_out[h] = state

        @pl.when(z == 0)
        def _():
            f_in[h] = jnp.zeros((WIDTH, WIDTH), f32)
            forward(h).start()
        return carry

    lax.fori_loop(0, heads, states, 0)

    def device_total(h):
        result = total(h, 0)
        for b in range(1, count):
            result = result + total(h, b)
        return result

    def attend(h):
        load(2, h).wait()
        load(3, h).wait()
        for b in range(count):
            at = pl.ds(b * size, size)
            wide = jnp.concatenate([cols_g[at, cols(h)]] * (size // WIDTH), axis=1)
            m = jnp.exp(jnp.where(below, wide - sums_g[pl.ds(h, 1), at], -1e30))
            mask[h, at, :] = m
            high, low = split(dot(q[at, cols(h)], k[at, cols(h)], 1, 1) * m)
            p_high[h, at, :] = high.T
            p_low[h, at, :] = low.T
            attn[at, cols(h)] = dot(high, v[at, cols(h)]) + dot(low, v[at, cols(h)])

    def enter(h):
        @pl.when(z > 0)
        def _():
            forward(h).wait_recv()

            @pl.when(z < seq_count - 1)
            def _():
                f_out[h] = f_out[h] + jnp.exp(device_total(h)) * f_in[h]
                forward(h).start()

        state = f_in[h]
        for b in range(count):
            at = pl.ds(b * size, size)
            entering[h, b] = state
            high, low = split(state)
            query = q[at, cols(h)]
            cross = dot(jnp.concatenate([query, query], axis=1), jnp.concatenate([high, low], axis=0))
            value = attn[at, cols(h)] + jnp.exp(cols_g[at, cols(h)]) * cross
            attn[at, cols(h)] = value
            acc_sq[at, :] = acc_sq[at, :] + value * value
            acc_pr[at, :] = acc_pr[at, :] + value * (g[at, cols(h)].astype(f32) * gain[:, cols(h)])
            state = jnp.exp(total(h, b)) * state + own[h, b]

    lag = jnp.where(z == 0, 0, jnp.minimum(heads, 3 * z - 1))

    def forward_step(i, carry):
        @pl.when(i < heads)
        def _():
            attend(i)

        @pl.when(i >= lag)
        def _():
            enter(i - lag)
        return carry

    lax.fori_loop(0, heads + lag, forward_step, 0)

    for b in range(rows // WIDTH):
        at = pl.ds(b * WIDTH, WIDTH)
        norm[me, 0:1, at] = jnp.sum(acc_sq[at, :].T, axis=0, keepdims=True)
        norm[me, 1:2, at] = jnp.sum(acc_pr[at, :].T, axis=0, keepdims=True)

    def exchange(step):
        return pltpu.make_async_remote_copy(
            src_ref=norm.at[me], dst_ref=norm.at[me], send_sem=n_send.at[step], recv_sem=n_recv.at[step],
            device_id=(z, lax.rem(me + step, head_count)), device_id_type=MESH)

    def arrived(step):
        slot = norm.at[lax.rem(me + head_count - step, head_count)]
        return pltpu.make_async_remote_copy(
            src_ref=slot, dst_ref=slot, send_sem=n_send.at[step], recv_sem=n_recv.at[step],
            device_id=(z, lax.rem(me + step, head_count)), device_id_type=MESH)

    for step in range(1, head_count):
        exchange(step).start()
    for step in range(1, head_count):
        arrived(step).wait_recv()
    summed = norm[0]
    for d in range(1, head_count):
        summed = summed + norm[d]
    inverse = 1.0 / jnp.sqrt(summed[0:1] / channels + epsilon)
    second = inverse * inverse * inverse * (summed[1:2] / channels)
    for b in range(rows // WIDTH):
        at = slice(b * WIDTH, (b + 1) * WIDTH)
        alpha[at, :] = jnp.broadcast_to(inverse[:, at], (WIDTH, WIDTH)).T
        beta[at, :] = jnp.broadcast_to(second[:, at], (WIDTH, WIDTH)).T

    def gradients(h, carry):
        gain_h = gain[:, cols(h)]
        part = jnp.zeros((1, WIDTH), f32)
        state = jnp.zeros((WIDTH, WIDTH), f32)
        for b in reversed(range(count)):
            at = pl.ds(b * size, size)
            scale = alpha[at, :]
            value = attn[at, cols(h)]
            cotangent = g[at, cols(h)].astype(f32)
            normed = value * scale
            out[at, cols(h)] = (normed * gain_h).astype(bf16)
            part = part + jnp.sum(cotangent * normed, axis=0, keepdims=True)
            a = scale * (cotangent * gain_h) - beta[at, :] * value
            attn[at, cols(h)] = a
            high, low = split(a * jnp.exp(cols_g[at, cols(h)]))
            both = dot(q[at, cols(h)], jnp.concatenate([high, low], axis=1), 0, 0)
            mine = both[:, :WIDTH] + both[:, WIDTH:]
            back[h, b] = mine
            state = jnp.exp(total(h, b)) * state + mine
        gparts[z, :, cols(h)] = part
        b_out[h] = state
        store(0, h).start()

        @pl.when(z == seq_count - 1)
        def _():
            b_in[h] = jnp.zeros((WIDTH, WIDTH), f32)
            backward(h).start()
        return carry

    lax.fori_loop(0, heads, gradients, 0)

    def gain_copy(step, slot):
        return pltpu.make_async_remote_copy(
            src_ref=gparts.at[slot], dst_ref=gparts.at[slot], send_sem=g_send.at[step], recv_sem=g_recv.at[step],
            device_id=(lax.rem(z + step, seq_count), me), device_id_type=MESH)

    for step in range(1, seq_count):
        gain_copy(step, z).start()

    def relay(h):
        backward(h).wait_recv()
        b_out[h] = b_out[h] + jnp.exp(device_total(h)) * b_in[h]
        backward(h).start()

    def inside_gradients(h):
        for b in range(count):
            at = pl.ds(b * size, size)
            query, key, value = q[at, cols(h)], k[at, cols(h)], v[at, cols(h)]
            a_high, a_low = split(attn[at, cols(h)])
            a_both = jnp.concatenate([a_high, a_low], axis=1)
            ds = dot(a_both, jnp.concatenate([value, value], axis=1), 1, 1) * mask[h, at, :]
            ds_high, ds_low = split(ds)
            column = cols_g[at, cols(h)]
            e_high, e_low = split(entering[h, b])
            cross = dot(a_both, jnp.concatenate([e_high, e_high], axis=1), 1, 1) + dot(a_high, e_low, 1, 1)
            dq[at, cols(h)] = (
                dot(ds_high, key) + dot(ds_low, key) + jnp.exp(column) * cross
            ).astype(bf16)
            mask[h, at, 0:WIDTH] = dot(ds_high, query, 0, 0) + dot(ds_low, query, 0, 0)
            both = dot(p_high[h, at, :], a_both)
            mask[h, at, WIDTH:2 * WIDTH] = both[:, :WIDTH] + both[:, WIDTH:] + dot(p_low[h, at, :], a_high)
        store(1, h).start()

    def leave(h):
        @pl.when(z == 0)
        def _():
            backward(h).wait_recv()

        state = b_in[h]
        for b in reversed(range(count)):
            at = pl.ds(b * size, size)
            key, value = k[at, cols(h)], v[at, cols(h)]
            to_end = jnp.exp(total(h, b) - cols_g[at, cols(h)])
            s_high, s_low = split(state)
            from_later = dot(jnp.concatenate([value, value], axis=1), jnp.concatenate([s_high, s_low], axis=1), 1, 1)
            dk[at, cols(h)] = (mask[h, at, 0:WIDTH] + to_end * from_later).astype(bf16)
            from_later = dot(jnp.concatenate([key, key], axis=1), jnp.concatenate([s_high, s_low], axis=0))
            dv[at, cols(h)] = (mask[h, at, WIDTH:2 * WIDTH] + to_end * from_later).astype(bf16)
            state = jnp.exp(total(h, b)) * state + back[h, b]
        store(2, h).start()
        store(3, h).start()

    late = jnp.where(z == seq_count - 1, 0, jnp.minimum(heads, 1 + 2 * (seq_count - 2 - z)))
    between = jnp.logical_and(z > 0, z < seq_count - 1)

    def backward_step(i, carry):
        for r in range(2):
            j = 2 * (i - late) + r

            @pl.when(jnp.logical_and(between, jnp.logical_and(j >= 0, j < heads)))
            def _():
                relay(j)

        @pl.when(i < heads)
        def _():
            inside_gradients(i)

        @pl.when(i >= late)
        def _():
            leave(i - late)
        return carry

    lax.fori_loop(0, heads + late, backward_step, 0)

    for step in range(1, seq_count):
        gain_copy(step, lax.rem(z + seq_count - step, seq_count)).wait_recv()
    result = gparts[0]
    for d in range(1, seq_count):
        result = result + gparts[d]
    dgain[...] = result

    for step in range(1, seq_count):
        gain_copy(step, z).wait_send()
    for step in range(1, head_count):
        exchange(step).wait_send()
    for h in range(heads):
        for n in range(4):
            store(n, h).wait()

    @pl.when(z < seq_count - 1)
    def _():
        for h in range(heads):
            forward(h).wait_send()

    @pl.when(z > 0)
    def _():
        for h in range(heads):
            backward(h).wait_send()


def local(queries, keys, values, log_decay, gain, out_grad):
    rows, channels = queries.shape
    heads = log_decay.shape[0]
    seq_count, head_count = lax.axis_size("seq"), lax.axis_size("head")
    size = min(256, rows)
    count = rows // size
    any_spec = pl.BlockSpec(memory_space=pl.ANY)
    vmem_spec = pl.BlockSpec(memory_space=pltpu.VMEM)
    narrow = jax.ShapeDtypeStruct((rows, channels), bf16)
    state = pltpu.VMEM((heads, WIDTH, WIDTH), f32)
    block_states = pltpu.VMEM((heads, count, WIDTH, WIDTH), f32)
    dma = pltpu.SemaphoreType.DMA
    results = pl.pallas_call(
        functools.partial(kernel, seq_count, head_count, heads, rows),
        out_shape=(narrow,) * 4 + (jax.ShapeDtypeStruct((1, channels), f32),),
        in_specs=[vmem_spec, vmem_spec] + [any_spec] * 4,
        out_specs=(any_spec,) * 4 + (vmem_spec,),
        scratch_shapes=[pltpu.VMEM((rows, channels), bf16)] * 8
        + [
            pltpu.VMEM((rows, channels), f32),
            pltpu.VMEM((heads, rows), f32),
            pltpu.VMEM((rows, channels), f32),
            block_states, block_states, block_states,
            pltpu.VMEM((heads, rows, size), f32),
            pltpu.VMEM((heads, rows, size), bf16),
            pltpu.VMEM((heads, rows, size), bf16),
            state, state, state, state,
            pltpu.VMEM((rows, WIDTH), f32),
            pltpu.VMEM((rows, WIDTH), f32),
            pltpu.VMEM((head_count, 2, rows), f32),
            pltpu.VMEM((rows, WIDTH), f32),
            pltpu.VMEM((rows, WIDTH), f32),
            pltpu.VMEM((seq_count, 1, channels), f32),
            dma((4, heads)), dma((4, heads)),
            dma((heads,)), dma((heads,)), dma((heads,)), dma((heads,)),
            dma((head_count,)), dma((head_count,)), dma((seq_count,)), dma((seq_count,)),
        ],
        compiler_params=pltpu.CompilerParams(
            collective_id=0, has_side_effects=True, vmem_limit_bytes=60 * 1024 * 1024
        ),
        name="lightning",
    )(log_decay, gain.reshape(1, channels), queries, keys, values, out_grad)
    return results[:4] + (results[4].reshape(channels),)


def solution(mesh):
    in_specs = (
        P("seq", "head"),
        P("seq", "head"),
        P("seq", "head"),
        P("head", "seq"),
        P("head"),
        P("seq", "head"),
    )
    out_specs = (P("seq", "head"), P("seq", "head"), P("seq", "head"), P("seq", "head"), P("head"))
    return jax.shard_map(local, mesh=mesh, in_specs=in_specs, out_specs=out_specs, check_vma=False)
```

```python
import functools

import jax
import jax.numpy as jnp
from jax import lax
from jax.experimental import pallas as pl
from jax.experimental.pallas import tpu as pltpu
from jax.sharding import PartitionSpec as P

epsilon = 1e-06
highest = lax.Precision.HIGHEST
MESH = pl.DeviceIdType.MESH
WIDTH = 128
f32, bf16 = jnp.float32, jnp.bfloat16


def dot(a, b, ca=1, cb=0):
    return lax.dot_general(a, b, (((ca,), (cb,)), ((), ())), preferred_element_type=f32)


def split(x):
    high = x.astype(bf16)
    return high, (x - high.astype(f32)).astype(bf16)


def kernel(
    seq_count, head_count, heads, rows,
    decay, gain, q_hbm, k_hbm, v_hbm, g_hbm,
    out_hbm, dq_hbm, dk_hbm, dv_hbm, dgain,
    q, k, v, g, out, dq, dk, dv,
    attn, sums_g, cols_g, ends, own, entering, back, mask, p_high, p_low,
    f_in, f_out, b_in, b_out, acc_sq, acc_pr, norm, alpha, beta, gparts,
    in_sem, out_sem, f_send, f_recv, b_send, b_recv, n_send, n_recv, g_send, g_recv,
):
    z = lax.axis_index("seq")
    me = lax.axis_index("head")
    size = min(128, rows)
    count = rows // size
    channels = heads * WIDTH * head_count

    def cols(h):
        return pl.ds(pl.multiple_of(h * WIDTH, WIDTH), WIDTH)

    def load(n, h):
        hbm, ref = ((k_hbm, k), (v_hbm, v), (q_hbm, q), (g_hbm, g))[n]
        return pltpu.make_async_copy(hbm.at[:, cols(h)], ref.at[:, cols(h)], in_sem.at[n, h])

    def store(n, h):
        hbm, ref = ((out_hbm, out), (dq_hbm, dq), (dk_hbm, dk), (dv_hbm, dv))[n]
        return pltpu.make_async_copy(ref.at[:, cols(h)], hbm.at[:, cols(h)], out_sem.at[n, h])

    def forward(h):
        return pltpu.make_async_remote_copy(
            src_ref=f_out.at[h], dst_ref=f_in.at[h], send_sem=f_send.at[h], recv_sem=f_recv.at[h],
            device_id=(lax.rem(z + 1, seq_count), me), device_id_type=MESH)

    def backward(h):
        return pltpu.make_async_remote_copy(
            src_ref=b_out.at[h], dst_ref=b_in.at[h], send_sem=b_send.at[h], recv_sem=b_recv.at[h],
            device_id=(lax.rem(z + seq_count - 1, seq_count), me), device_id_type=MESH)

    for h in range(heads):
        load(0, h).start()
        load(1, h).start()
    for h in range(heads):
        load(2, h).start()
        load(3, h).start()

    barrier = pltpu.get_barrier_semaphore()
    for step in range(1, head_count):
        pl.semaphore_signal(barrier, inc=1, device_id=(z, lax.rem(me + step, head_count)), device_id_type=MESH)
    for step in range(1, seq_count):
        pl.semaphore_signal(barrier, inc=1, device_id=(lax.rem(z + step, seq_count), me), device_id_type=MESH)

    below = lax.broadcasted_iota(jnp.int32, (size, size), 0) >= lax.broadcasted_iota(jnp.int32, (size, size), 1)
    above = lax.broadcasted_iota(jnp.int32, (size, size), 0) <= lax.broadcasted_iota(jnp.int32, (size, size), 1)
    tri = jnp.where(above, 1.0, 0.0).astype(f32)
    for b in range(count):
        at = pl.ds(b * size, size)
        along = jnp.dot(decay[:, at], tri, precision=highest, preferred_element_type=f32)
        for h in range(heads):
            sums_g[h, :, at] = along[h:h + 1]
    acc_sq[...] = jnp.zeros_like(acc_sq)
    acc_pr[...] = jnp.zeros_like(acc_pr)
    pl.semaphore_wait(barrier, head_count - 1 + seq_count - 1)

    def factor(h, b):
        return cols_g[(b + 1) * size - 1:(b + 1) * size, cols(h)]

    def states(h, carry):
        load(0, h).wait()
        load(1, h).wait()
        state = jnp.zeros((WIDTH, WIDTH), f32)
        for b in range(count):
            at = pl.ds(b * size, size)
            column = jnp.broadcast_to(sums_g[h, :, at], (WIDTH, size)).T
            cols_g[at, cols(h)] = column
            last = column[size - 1:size, :]
            to_end = jnp.exp(last - column)
            ends[at, cols(h)] = to_end
            high, low = split(v[at, cols(h)].astype(f32) * to_end)
            both = dot(k[at, cols(h)], jnp.concatenate([high, low], axis=1), 0, 0)
            mine = both[:, :WIDTH] + both[:, WIDTH:]
            own[h, b] = mine
            state = jnp.exp(last) * state + mine
        f_out[h] = state

        @pl.when(z == 0)
        def _():
            f_in[h] = jnp.zeros((WIDTH, WIDTH), f32)
            forward(h).start()
        return carry

    lax.fori_loop(0, heads, states, 0)

    def device_factor(h):
        result = factor(h, 0)
        for b in range(1, count):
            result = result * factor(h, b)
        return result

    def attend(h):
        load(2, h).wait()
        load(3, h).wait()
        for b in range(count):
            at = pl.ds(b * size, size)
            column = cols_g[at, cols(h)]
            m = jnp.exp(jnp.where(below, column - sums_g[h, :, at], -1e30))
            cols_g[at, cols(h)] = jnp.exp(column)
            mask[h, at, :] = m
            high, low = split(dot(q[at, cols(h)], k[at, cols(h)], 1, 1) * m)
            p_high[h, at, :] = high.T
            p_low[h, at, :] = low.T
            value = v[at, cols(h)]
            attn[at, cols(h)] = dot(
                jnp.concatenate([high, low], axis=1), jnp.concatenate([value, value], axis=0)
            )

    def enter(h):
        @pl.when(z > 0)
        def _():
            forward(h).wait_recv()

            @pl.when(z < seq_count - 1)
            def _():
                f_out[h] = f_out[h] + device_factor(h) * f_in[h]
                forward(h).start()

        state = f_in[h]
        for b in range(count):
            at = pl.ds(b * size, size)
            entering[h, b] = state
            high, low = split(state)
            query = q[at, cols(h)]
            cross = dot(jnp.concatenate([query, query], axis=1), jnp.concatenate([high, low], axis=0))
            value = attn[at, cols(h)] + cols_g[at, cols(h)] * cross
            attn[at, cols(h)] = value
            acc_sq[at, :] = acc_sq[at, :] + value * value
            acc_pr[at, :] = acc_pr[at, :] + value * (g[at, cols(h)].astype(f32) * gain[:, cols(h)])
            state = factor(h, b) * state + own[h, b]

    lag = jnp.where(z == 0, 0, jnp.minimum(heads, 3 * z - 1))

    def forward_step(i, carry):
        @pl.when(i < heads)
        def _():
            attend(i)

        @pl.when(i >= lag)
        def _():
            enter(i - lag)
        return carry

    lax.fori_loop(0, heads + lag, forward_step, 0)

    for b in range(rows // WIDTH):
        at = pl.ds(b * WIDTH, WIDTH)
        norm[me, 0:1, at] = jnp.sum(acc_sq[at, :].T, axis=0, keepdims=True)
        norm[me, 1:2, at] = jnp.sum(acc_pr[at, :].T, axis=0, keepdims=True)

    def exchange(step):
        return pltpu.make_async_remote_copy(
            src_ref=norm.at[me], dst_ref=norm.at[me], send_sem=n_send.at[step], recv_sem=n_recv.at[step],
            device_id=(z, lax.rem(me + step, head_count)), device_id_type=MESH)

    def arrived(step):
        slot = norm.at[lax.rem(me + head_count - step, head_count)]
        return pltpu.make_async_remote_copy(
            src_ref=slot, dst_ref=slot, send_sem=n_send.at[step], recv_sem=n_recv.at[step],
            device_id=(z, lax.rem(me + step, head_count)), device_id_type=MESH)

    for step in range(1, head_count):
        exchange(step).start()
    for step in range(1, head_count):
        arrived(step).wait_recv()
    summed = norm[0]
    for d in range(1, head_count):
        summed = summed + norm[d]
    inverse = 1.0 / jnp.sqrt(summed[0:1] / channels + epsilon)
    second = inverse * inverse * inverse * (summed[1:2] / channels)
    for b in range(rows // WIDTH):
        at = slice(b * WIDTH, (b + 1) * WIDTH)
        alpha[at, :] = jnp.broadcast_to(inverse[:, at], (WIDTH, WIDTH)).T
        beta[at, :] = jnp.broadcast_to(second[:, at], (WIDTH, WIDTH)).T

    def gradients(h, carry):
        gain_h = gain[:, cols(h)]
        part = jnp.zeros((1, WIDTH), f32)
        state = jnp.zeros((WIDTH, WIDTH), f32)
        for b in reversed(range(count)):
            at = pl.ds(b * size, size)
            scale = alpha[at, :]
            value = attn[at, cols(h)]
            cotangent = g[at, cols(h)].astype(f32)
            normed = value * scale
            out[at, cols(h)] = (normed * gain_h).astype(bf16)
            part = part + jnp.sum(cotangent * normed, axis=0, keepdims=True)
            a = scale * (cotangent * gain_h) - beta[at, :] * value
            attn[at, cols(h)] = a
            high, low = split(a * cols_g[at, cols(h)])
            both = dot(q[at, cols(h)], jnp.concatenate([high, low], axis=1), 0, 0)
            mine = both[:, :WIDTH] + both[:, WIDTH:]
            back[h, b] = mine
            state = factor(h, b) * state + mine
        gparts[z, :, cols(h)] = part
        b_out[h] = state
        store(0, h).start()

        @pl.when(z == seq_count - 1)
        def _():
            b_in[h] = jnp.zeros((WIDTH, WIDTH), f32)
            backward(h).start()
        return carry

    lax.fori_loop(0, heads, gradients, 0)

    def gain_copy(step, slot):
        return pltpu.make_async_remote_copy(
            src_ref=gparts.at[slot], dst_ref=gparts.at[slot], send_sem=g_send.at[step], recv_sem=g_recv.at[step],
            device_id=(lax.rem(z + step, seq_count), me), device_id_type=MESH)

    for step in range(1, seq_count):
        gain_copy(step, z).start()

    def relay(h):
        backward(h).wait_recv()
        b_out[h] = b_out[h] + device_factor(h) * b_in[h]
        backward(h).start()

    def inside_gradients(h):
        for b in range(count):
            at = pl.ds(b * size, size)
            query, key, value = q[at, cols(h)], k[at, cols(h)], v[at, cols(h)]
            a_high, a_low = split(attn[at, cols(h)])
            a_both = jnp.concatenate([a_high, a_low], axis=1)
            e_high, e_low = split(entering[h, b])
            right = jnp.concatenate(
                [jnp.concatenate([value, value], axis=1), jnp.concatenate([e_high, e_high], axis=1)], axis=0
            )
            both = dot(a_both, right, 1, 1)
            ds_high, ds_low = split(both[:, :size] * mask[h, at, :])
            cross = both[:, size:] + dot(a_high, e_low, 1, 1)
            dq[at, cols(h)] = (
                dot(jnp.concatenate([ds_high, ds_low], axis=1), jnp.concatenate([key, key], axis=0))
                + cols_g[at, cols(h)] * cross
            ).astype(bf16)
            mask[h, at, :] = dot(
                jnp.concatenate([ds_high, ds_low], axis=0), jnp.concatenate([query, query], axis=0), 0, 0
            )
            right = jnp.concatenate(
                [a_both, jnp.concatenate([a_high, jnp.zeros_like(a_high)], axis=1)], axis=0
            )
            both = dot(jnp.concatenate([p_high[h, at, :], p_low[h, at, :]], axis=1), right)
            attn[at, cols(h)] = both[:, :WIDTH] + both[:, WIDTH:]
        store(1, h).start()

    def leave(h):
        @pl.when(z == 0)
        def _():
            backward(h).wait_recv()

        state = b_in[h]
        for b in reversed(range(count)):
            at = pl.ds(b * size, size)
            key, value = k[at, cols(h)], v[at, cols(h)]
            to_end = ends[at, cols(h)]
            s_high, s_low = split(state)
            from_later = dot(jnp.concatenate([value, value], axis=1), jnp.concatenate([s_high, s_low], axis=1), 1, 1)
            dk[at, cols(h)] = (mask[h, at, :] + to_end * from_later).astype(bf16)
            from_later = dot(jnp.concatenate([key, key], axis=1), jnp.concatenate([s_high, s_low], axis=0))
            dv[at, cols(h)] = (attn[at, cols(h)] + to_end * from_later).astype(bf16)
            state = factor(h, b) * state + back[h, b]
        store(2, h).start()
        store(3, h).start()

    late = jnp.where(z == seq_count - 1, 0, jnp.minimum(heads, 1 + 2 * (seq_count - 2 - z)))
    between = jnp.logical_and(z > 0, z < seq_count - 1)

    def backward_step(i, carry):
        for r in range(2):
            j = 2 * (i - late) + r

            @pl.when(jnp.logical_and(between, jnp.logical_and(j >= 0, j < heads)))
            def _():
                relay(j)

        @pl.when(i < heads)
        def _():
            inside_gradients(i)

        @pl.when(i >= late)
        def _():
            leave(i - late)
        return carry

    lax.fori_loop(0, heads + late, backward_step, 0)

    for step in range(1, seq_count):
        gain_copy(step, lax.rem(z + seq_count - step, seq_count)).wait_recv()
    result = gparts[0]
    for d in range(1, seq_count):
        result = result + gparts[d]
    dgain[...] = result

    for step in range(1, seq_count):
        gain_copy(step, z).wait_send()
    for step in range(1, head_count):
        exchange(step).wait_send()
    for h in range(heads):
        for n in range(4):
            store(n, h).wait()

    @pl.when(z < seq_count - 1)
    def _():
        for h in range(heads):
            forward(h).wait_send()

    @pl.when(z > 0)
    def _():
        for h in range(heads):
            backward(h).wait_send()


def local(queries, keys, values, log_decay, gain, out_grad):
    rows, channels = queries.shape
    heads = log_decay.shape[0]
    seq_count, head_count = lax.axis_size("seq"), lax.axis_size("head")
    size = min(128, rows)
    count = rows // size
    any_spec = pl.BlockSpec(memory_space=pl.ANY)
    vmem_spec = pl.BlockSpec(memory_space=pltpu.VMEM)
    narrow = jax.ShapeDtypeStruct((rows, channels), bf16)
    state = pltpu.VMEM((heads, WIDTH, WIDTH), f32)
    block_states = pltpu.VMEM((heads, count, WIDTH, WIDTH), f32)
    dma = pltpu.SemaphoreType.DMA
    results = pl.pallas_call(
        functools.partial(kernel, seq_count, head_count, heads, rows),
        out_shape=(narrow,) * 4 + (jax.ShapeDtypeStruct((1, channels), f32),),
        in_specs=[vmem_spec, vmem_spec] + [any_spec] * 4,
        out_specs=(any_spec,) * 4 + (vmem_spec,),
        scratch_shapes=[pltpu.VMEM((rows, channels), bf16)] * 8
        + [
            pltpu.VMEM((rows, channels), f32),
            pltpu.VMEM((heads, 1, rows), f32),
            pltpu.VMEM((rows, channels), f32),
            pltpu.VMEM((rows, channels), f32),
            block_states, block_states, block_states,
            pltpu.VMEM((heads, rows, size), f32),
            pltpu.VMEM((heads, rows, size), bf16),
            pltpu.VMEM((heads, rows, size), bf16),
            state, state, state, state,
            pltpu.VMEM((rows, WIDTH), f32),
            pltpu.VMEM((rows, WIDTH), f32),
            pltpu.VMEM((head_count, 2, rows), f32),
            pltpu.VMEM((rows, WIDTH), f32),
            pltpu.VMEM((rows, WIDTH), f32),
            pltpu.VMEM((seq_count, 1, channels), f32),
            dma((4, heads)), dma((4, heads)),
            dma((heads,)), dma((heads,)), dma((heads,)), dma((heads,)),
            dma((head_count,)), dma((head_count,)), dma((seq_count,)), dma((seq_count,)),
        ],
        compiler_params=pltpu.CompilerParams(
            collective_id=0, has_side_effects=True, vmem_limit_bytes=60 * 1024 * 1024
        ),
        name="lightning",
    )(log_decay, gain.reshape(1, channels), queries, keys, values, out_grad)
    return results[:4] + (results[4].reshape(channels),)


def solution(mesh):
    in_specs = (
        P("seq", "head"),
        P("seq", "head"),
        P("seq", "head"),
        P("head", "seq"),
        P("head"),
        P("seq", "head"),
    )
    out_specs = (P("seq", "head"), P("seq", "head"), P("seq", "head"), P("seq", "head"), P("head"))
    return jax.shard_map(local, mesh=mesh, in_specs=in_specs, out_specs=out_specs, check_vma=False)
```

```python
import functools

import jax
import jax.numpy as jnp
from jax import lax
from jax.experimental import pallas as pl
from jax.experimental.pallas import tpu as pltpu
from jax.sharding import PartitionSpec as P

epsilon = 1e-06
highest = lax.Precision.HIGHEST
MESH = pl.DeviceIdType.MESH
WIDTH = 128
f32, bf16 = jnp.float32, jnp.bfloat16


def dot(a, b, ca=1, cb=0):
    return lax.dot_general(a, b, (((ca,), (cb,)), ((), ())), preferred_element_type=f32)


def split(x):
    high = x.astype(bf16)
    return high, (x - high.astype(f32)).astype(bf16)


def kernel(
    seq_count, head_count, heads, rows,
    decay, gain, q_hbm, k_hbm, v_hbm, g_hbm,
    out_hbm, dq_hbm, dk_hbm, dv_hbm, dgain,
    q, k, v, g, out, dq, dk, dv,
    attn, sums_g, cols_g, ends, own, entering, back, mask, p_high, p_low,
    f_in, f_out, b_in, b_out, acc_sq, acc_pr, norm, alpha, beta, gparts,
    in_sem, out_sem, f_send, f_recv, b_send, b_recv, n_send, n_recv, g_send, g_recv,
):
    z = lax.axis_index("seq")
    me = lax.axis_index("head")
    size = min(256, rows)
    count = rows // size
    channels = heads * WIDTH * head_count

    spans = [pl.ds(b * size, size) for b in range(count)]
    blocks = range(count)

    def halves(x):
        return x[:, :WIDTH] + x[:, WIDTH:]

    def cols(h):
        return pl.ds(pl.multiple_of(h * WIDTH, WIDTH), WIDTH)

    def load(n, h):
        hbm, ref = ((k_hbm, k), (v_hbm, v), (q_hbm, q), (g_hbm, g))[n]
        return pltpu.make_async_copy(hbm.at[:, cols(h)], ref.at[:, cols(h)], in_sem.at[n, h])

    def store(n, h):
        hbm, ref = ((out_hbm, out), (dq_hbm, dq), (dk_hbm, dk), (dv_hbm, dv))[n]
        return pltpu.make_async_copy(ref.at[:, cols(h)], hbm.at[:, cols(h)], out_sem.at[n, h])

    def forward(h):
        return pltpu.make_async_remote_copy(
            src_ref=f_out.at[h], dst_ref=f_in.at[h], send_sem=f_send.at[h], recv_sem=f_recv.at[h],
            device_id=(lax.rem(z + 1, seq_count), me), device_id_type=MESH)

    def backward(h):
        return pltpu.make_async_remote_copy(
            src_ref=b_out.at[h], dst_ref=b_in.at[h], send_sem=b_send.at[h], recv_sem=b_recv.at[h],
            device_id=(lax.rem(z + seq_count - 1, seq_count), me), device_id_type=MESH)

    for h in range(heads):
        load(0, h).start()
        load(1, h).start()
    for h in range(heads):
        load(2, h).start()
        load(3, h).start()

    barrier = pltpu.get_barrier_semaphore()
    for step in range(1, head_count):
        pl.semaphore_signal(barrier, inc=1, device_id=(z, lax.rem(me + step, head_count)), device_id_type=MESH)
    for step in range(1, seq_count):
        pl.semaphore_signal(barrier, inc=1, device_id=(lax.rem(z + step, seq_count), me), device_id_type=MESH)

    below = lax.broadcasted_iota(jnp.int32, (size, size), 0) >= lax.broadcasted_iota(jnp.int32, (size, size), 1)
    above = lax.broadcasted_iota(jnp.int32, (size, size), 0) <= lax.broadcasted_iota(jnp.int32, (size, size), 1)
    tri = jnp.where(above, 1.0, 0.0).astype(f32)
    for b in range(count):
        at = pl.ds(b * size, size)
        along = jnp.dot(decay[:, at], tri, precision=highest, preferred_element_type=f32)
        for h in range(heads):
            sums_g[h, :, at] = along[h:h + 1]
    acc_sq[...] = jnp.zeros_like(acc_sq)
    acc_pr[...] = jnp.zeros_like(acc_pr)
    pl.semaphore_wait(barrier, head_count - 1 + seq_count - 1)

    def factor(h, b):
        return cols_g[(b + 1) * size - 1:(b + 1) * size, cols(h)]

    def states(h, carry):
        load(0, h).wait()
        load(1, h).wait()
        values = [v[at, cols(h)].astype(f32) for at in spans]
        key_blocks = [k[at, cols(h)] for at in spans]
        columns = [jnp.broadcast_to(sums_g[h, :, at], (WIDTH, size)).T for at in spans]
        lasts = [column[size - 1:size, :] for column in columns]
        to_ends = [jnp.exp(lasts[b] - columns[b]) for b in blocks]
        sides = [jnp.concatenate(split(values[b] * to_ends[b]), axis=1) for b in blocks]
        mine = [halves(dot(key_blocks[b], sides[b], 0, 0)) for b in blocks]
        state = jnp.zeros((WIDTH, WIDTH), f32)
        for b in blocks:
            state = jnp.exp(lasts[b]) * state + mine[b]
        for b in blocks:
            cols_g[spans[b], cols(h)] = columns[b]
            ends[spans[b], cols(h)] = to_ends[b]
            own[h, b] = mine[b]
        f_out[h] = state

        @pl.when(z == 0)
        def _():
            f_in[h] = jnp.zeros((WIDTH, WIDTH), f32)
            forward(h).start()
        return carry

    lax.fori_loop(0, heads, states, 0)

    def device_factor(h):
        result = factor(h, 0)
        for b in range(1, count):
            result = result * factor(h, b)
        return result

    def attend(h):
        load(2, h).wait()
        load(3, h).wait()
        columns = [cols_g[at, cols(h)] for at in spans]
        across = [sums_g[h, :, at] for at in spans]
        query_blocks = [q[at, cols(h)] for at in spans]
        key_blocks = [k[at, cols(h)] for at in spans]
        value_blocks = [v[at, cols(h)] for at in spans]
        scores = [dot(query_blocks[b], key_blocks[b], 1, 1) for b in blocks]
        masks = [
            jnp.exp(jnp.where(below, jnp.concatenate([columns[b]] * (size // WIDTH), axis=1) - across[b], -1e30))
            for b in blocks
        ]
        parts = [split(scores[b] * masks[b]) for b in blocks]
        inside = [dot(parts[b][0], value_blocks[b]) + dot(parts[b][1], value_blocks[b]) for b in blocks]
        for b in blocks:
            at = spans[b]
            mask[h, at, :] = masks[b]
            p_high[h, at, :] = parts[b][0].T
            p_low[h, at, :] = parts[b][1].T
            attn[at, cols(h)] = inside[b]
            cols_g[at, cols(h)] = jnp.exp(columns[b])

    def enter(h):
        @pl.when(z > 0)
        def _():
            forward(h).wait_recv()

            @pl.when(z < seq_count - 1)
            def _():
                f_out[h] = f_out[h] + device_factor(h) * f_in[h]
                forward(h).start()

        state = f_in[h]
        factors = [factor(h, b) for b in blocks]
        own_blocks = [own[h, b] for b in blocks]
        query_blocks = [q[at, cols(h)] for at in spans]
        inside = [attn[at, cols(h)] for at in spans]
        starts = [cols_g[at, cols(h)] for at in spans]
        weights = [g[at, cols(h)].astype(f32) * gain[:, cols(h)] for at in spans]
        before = []
        for b in blocks:
            before.append(state)
            state = factors[b] * state + own_blocks[b]
        crosses = [
            dot(jnp.concatenate([query_blocks[b]] * 2, axis=1), jnp.concatenate(split(before[b]), axis=0))
            for b in blocks
        ]
        results = [inside[b] + starts[b] * crosses[b] for b in blocks]
        for b in blocks:
            at = spans[b]
            entering[h, b] = before[b]
            attn[at, cols(h)] = results[b]
            acc_sq[at, :] = acc_sq[at, :] + results[b] * results[b]
            acc_pr[at, :] = acc_pr[at, :] + results[b] * weights[b]

    lag = jnp.where(z == 0, 0, jnp.minimum(heads, 3 * z - 1))

    def forward_step(i, carry):
        @pl.when(i < heads)
        def _():
            attend(i)

        @pl.when(i >= lag)
        def _():
            enter(i - lag)
        return carry

    lax.fori_loop(0, heads + lag, forward_step, 0)

    for b in range(rows // WIDTH):
        at = pl.ds(b * WIDTH, WIDTH)
        norm[me, 0:1, at] = jnp.sum(acc_sq[at, :].T, axis=0, keepdims=True)
        norm[me, 1:2, at] = jnp.sum(acc_pr[at, :].T, axis=0, keepdims=True)

    def exchange(step):
        return pltpu.make_async_remote_copy(
            src_ref=norm.at[me], dst_ref=norm.at[me], send_sem=n_send.at[step], recv_sem=n_recv.at[step],
            device_id=(z, lax.rem(me + step, head_count)), device_id_type=MESH)

    def arrived(step):
        slot = norm.at[lax.rem(me + head_count - step, head_count)]
        return pltpu.make_async_remote_copy(
            src_ref=slot, dst_ref=slot, send_sem=n_send.at[step], recv_sem=n_recv.at[step],
            device_id=(z, lax.rem(me + step, head_count)), device_id_type=MESH)

    for step in range(1, head_count):
        exchange(step).start()
    for step in range(1, head_count):
        arrived(step).wait_recv()
    summed = norm[0]
    for d in range(1, head_count):
        summed = summed + norm[d]
    inverse = 1.0 / jnp.sqrt(summed[0:1] / channels + epsilon)
    second = inverse * inverse * inverse * (summed[1:2] / channels)
    for b in range(rows // WIDTH):
        at = slice(b * WIDTH, (b + 1) * WIDTH)
        alpha[at, :] = jnp.broadcast_to(inverse[:, at], (WIDTH, WIDTH)).T
        beta[at, :] = jnp.broadcast_to(second[:, at], (WIDTH, WIDTH)).T

    def gradients(h, carry):
        gain_h = gain[:, cols(h)]
        part = jnp.zeros((1, WIDTH), f32)
        state = jnp.zeros((WIDTH, WIDTH), f32)
        factors = [factor(h, b) for b in blocks]
        scales = [alpha[at, :] for at in spans]
        seconds = [beta[at, :] for at in spans]
        attended = [attn[at, cols(h)] for at in spans]
        cotangents = [g[at, cols(h)].astype(f32) for at in spans]
        starts = [cols_g[at, cols(h)] for at in spans]
        query_blocks = [q[at, cols(h)] for at in spans]
        grads = [
            scales[b] * (cotangents[b] * gain_h) - seconds[b] * attended[b] for b in blocks
        ]
        sides = [jnp.concatenate(split(grads[b] * starts[b]), axis=1) for b in blocks]
        mine = [halves(dot(query_blocks[b], sides[b], 0, 0)) for b in blocks]
        normed = [attended[b] * scales[b] for b in blocks]
        for b in reversed(blocks):
            part = part + jnp.sum(cotangents[b] * normed[b], axis=0, keepdims=True)
            state = factors[b] * state + mine[b]
        for b in blocks:
            at = spans[b]
            out[at, cols(h)] = (normed[b] * gain_h).astype(bf16)
            attn[at, cols(h)] = grads[b]
            back[h, b] = mine[b]
        gparts[z, :, cols(h)] = part
        b_out[h] = state
        store(0, h).start()

        @pl.when(z == seq_count - 1)
        def _():
            b_in[h] = jnp.zeros((WIDTH, WIDTH), f32)
            backward(h).start()
        return carry

    lax.fori_loop(0, heads, gradients, 0)

    def gain_copy(step, slot):
        return pltpu.make_async_remote_copy(
            src_ref=gparts.at[slot], dst_ref=gparts.at[slot], send_sem=g_send.at[step], recv_sem=g_recv.at[step],
            device_id=(lax.rem(z + step, seq_count), me), device_id_type=MESH)

    for step in range(1, seq_count):
        gain_copy(step, z).start()

    def relay(h):
        backward(h).wait_recv()
        b_out[h] = b_out[h] + device_factor(h) * b_in[h]
        backward(h).start()

    def inside_gradients(h):
        query_blocks = [q[at, cols(h)] for at in spans]
        key_blocks = [k[at, cols(h)] for at in spans]
        value_blocks = [v[at, cols(h)] for at in spans]
        parts = [split(attn[at, cols(h)]) for at in spans]
        masks = [mask[h, at, :] for at in spans]
        starts = [cols_g[at, cols(h)] for at in spans]
        states_in = [split(entering[h, b]) for b in blocks]
        highs = [p_high[h, at, :] for at in spans]
        lows = [p_low[h, at, :] for at in spans]
        both = [jnp.concatenate(parts[b], axis=1) for b in blocks]
        score_grads = [
            split(dot(both[b], jnp.concatenate([value_blocks[b]] * 2, axis=1), 1, 1) * masks[b]) for b in blocks
        ]
        crosses = [
            dot(both[b], jnp.concatenate([states_in[b][0]] * 2, axis=1), 1, 1)
            + dot(parts[b][0], states_in[b][1], 1, 1)
            for b in blocks
        ]
        value_parts = [halves(dot(highs[b], both[b])) + dot(lows[b], parts[b][0]) for b in blocks]
        query_parts = [
            dot(score_grads[b][0], key_blocks[b]) + dot(score_grads[b][1], key_blocks[b]) + starts[b] * crosses[b]
            for b in blocks
        ]
        key_parts = [
            dot(score_grads[b][0], query_blocks[b], 0, 0) + dot(score_grads[b][1], query_blocks[b], 0, 0)
            for b in blocks
        ]
        for b in blocks:
            at = spans[b]
            dq[at, cols(h)] = query_parts[b].astype(bf16)
            mask[h, at, 0:WIDTH] = key_parts[b]
            attn[at, cols(h)] = value_parts[b]
        store(1, h).start()

    def leave(h):
        @pl.when(z == 0)
        def _():
            backward(h).wait_recv()

        state = b_in[h]
        factors = [factor(h, b) for b in blocks]
        back_blocks = [back[h, b] for b in blocks]
        key_blocks = [k[at, cols(h)] for at in spans]
        value_blocks = [v[at, cols(h)] for at in spans]
        to_ends = [ends[at, cols(h)] for at in spans]
        key_parts = [mask[h, at, 0:WIDTH] for at in spans]
        value_parts = [attn[at, cols(h)] for at in spans]
        after = [None] * count
        for b in reversed(blocks):
            after[b] = split(state)
            state = factors[b] * state + back_blocks[b]
        from_values = [
            dot(jnp.concatenate([value_blocks[b]] * 2, axis=1), jnp.concatenate(after[b], axis=1), 1, 1) for b in blocks
        ]
        from_keys = [
            dot(jnp.concatenate([key_blocks[b]] * 2, axis=1), jnp.concatenate(after[b], axis=0)) for b in blocks
        ]
        for b in blocks:
            at = spans[b]
            dk[at, cols(h)] = (key_parts[b] + to_ends[b] * from_values[b]).astype(bf16)
            dv[at, cols(h)] = (value_parts[b] + to_ends[b] * from_keys[b]).astype(bf16)
        store(2, h).start()
        store(3, h).start()

    late = jnp.where(z == seq_count - 1, 0, jnp.minimum(heads, 1 + 2 * (seq_count - 2 - z)))
    between = jnp.logical_and(z > 0, z < seq_count - 1)

    def backward_step(i, carry):
        for r in range(2):
            j = 2 * (i - late) + r

            @pl.when(jnp.logical_and(between, jnp.logical_and(j >= 0, j < heads)))
            def _():
                relay(j)

        @pl.when(i < heads)
        def _():
            inside_gradients(i)

        @pl.when(i >= late)
        def _():
            leave(i - late)
        return carry

    lax.fori_loop(0, heads + late, backward_step, 0)

    for step in range(1, seq_count):
        gain_copy(step, lax.rem(z + seq_count - step, seq_count)).wait_recv()
    result = gparts[0]
    for d in range(1, seq_count):
        result = result + gparts[d]
    dgain[...] = result

    for step in range(1, seq_count):
        gain_copy(step, z).wait_send()
    for step in range(1, head_count):
        exchange(step).wait_send()
    for h in range(heads):
        for n in range(4):
            store(n, h).wait()

    @pl.when(z < seq_count - 1)
    def _():
        for h in range(heads):
            forward(h).wait_send()

    @pl.when(z > 0)
    def _():
        for h in range(heads):
            backward(h).wait_send()


def hand_on(rows, *refs):
    sources, targets, sem = refs[:5], refs[5:10], refs[10]
    pieces = 8
    step = rows // pieces
    copies = []
    for n in range(4):
        for p in range(pieces):
            at = pl.ds(p * step, step)
            copies.append(pltpu.make_async_copy(sources[n].at[at], targets[n].at[at], sem.at[n, p]))
    for copy in copies:
        copy.start()
    targets[4][...] = sources[4][...]
    for copy in copies:
        copy.wait()


def local(queries, keys, values, log_decay, gain, out_grad):
    rows, channels = queries.shape
    heads = log_decay.shape[0]
    seq_count, head_count = lax.axis_size("seq"), lax.axis_size("head")
    size = min(256, rows)
    count = rows // size
    any_spec = pl.BlockSpec(memory_space=pl.ANY)
    vmem_spec = pl.BlockSpec(memory_space=pltpu.VMEM)
    narrow = jax.ShapeDtypeStruct((rows, channels), bf16)
    state = pltpu.VMEM((heads, WIDTH, WIDTH), f32)
    block_states = pltpu.VMEM((heads, count, WIDTH, WIDTH), f32)
    dma = pltpu.SemaphoreType.DMA
    results = pl.pallas_call(
        functools.partial(kernel, seq_count, head_count, heads, rows),
        out_shape=(narrow,) * 4 + (jax.ShapeDtypeStruct((1, channels), f32),),
        in_specs=[vmem_spec, vmem_spec] + [any_spec] * 4,
        out_specs=(any_spec,) * 4 + (vmem_spec,),
        scratch_shapes=[pltpu.VMEM((rows, channels), bf16)] * 8
        + [
            pltpu.VMEM((rows, channels), f32),
            pltpu.VMEM((heads, 1, rows), f32),
            pltpu.VMEM((rows, channels), f32),
            pltpu.VMEM((rows, channels), f32),
            block_states, block_states, block_states,
            pltpu.VMEM((heads, rows, size), f32),
            pltpu.VMEM((heads, rows, size), bf16),
            pltpu.VMEM((heads, rows, size), bf16),
            state, state, state, state,
            pltpu.VMEM((rows, WIDTH), f32),
            pltpu.VMEM((rows, WIDTH), f32),
            pltpu.VMEM((head_count, 2, rows), f32),
            pltpu.VMEM((rows, WIDTH), f32),
            pltpu.VMEM((rows, WIDTH), f32),
            pltpu.VMEM((seq_count, 1, channels), f32),
            dma((4, heads)), dma((4, heads)),
            dma((heads,)), dma((heads,)), dma((heads,)), dma((heads,)),
            dma((head_count,)), dma((head_count,)), dma((seq_count,)), dma((seq_count,)),
        ],
        compiler_params=pltpu.CompilerParams(
            collective_id=0, has_side_effects=True, vmem_limit_bytes=60 * 1024 * 1024
        ),
        name="lightning",
    )(log_decay, gain.reshape(1, channels), queries, keys, values, out_grad)
    results = pl.pallas_call(
        functools.partial(hand_on, rows),
        out_shape=(narrow,) * 4 + (jax.ShapeDtypeStruct((1, channels), f32),),
        in_specs=[any_spec] * 4 + [vmem_spec],
        out_specs=(any_spec,) * 4 + (vmem_spec,),
        scratch_shapes=[dma((4, 8))],
        compiler_params=pltpu.CompilerParams(vmem_limit_bytes=60 * 1024 * 1024),
        name="hand_on",
    )(*results)
    return results[:4] + (results[4].reshape(channels),)


def solution(mesh):
    in_specs = (
        P("seq", "head"),
        P("seq", "head"),
        P("seq", "head"),
        P("head", "seq"),
        P("head"),
        P("seq", "head"),
    )
    out_specs = (P("seq", "head"), P("seq", "head"), P("seq", "head"), P("seq", "head"), P("head"))
    return jax.shard_map(local, mesh=mesh, in_specs=in_specs, out_specs=out_specs, check_vma=False)
```

```python
import functools

import jax
import jax.numpy as jnp
from jax import lax
from jax.experimental import pallas as pl
from jax.experimental.pallas import tpu as pltpu
from jax.sharding import PartitionSpec as P

epsilon = 1e-06
highest = lax.Precision.HIGHEST
MESH = pl.DeviceIdType.MESH
WIDTH = 128
f32, bf16 = jnp.float32, jnp.bfloat16


def dot(a, b, ca=1, cb=0):
    return lax.dot_general(a, b, (((ca,), (cb,)), ((), ())), preferred_element_type=f32)


def split(x):
    high = x.astype(bf16)
    return high, (x - high.astype(f32)).astype(bf16)


def kernel(
    seq_count, head_count, heads, rows,
    decay, gain, q_hbm, k_hbm, v_hbm, g_hbm,
    out_hbm, dq_hbm, dk_hbm, dv_hbm, dgain,
    q, k, v, g, out, dq, dk, dv,
    attn, sums_g, cols_g, ends, own, entering, back, mask, p_high, p_low,
    decays, f_in, f_out, b_in, b_out, acc_sq, acc_pr, norm, alpha, beta, gparts,
    in_sem, out_sem, f_send, f_recv, b_send, b_recv, n_send, n_recv, g_send, g_recv,
):
    z = lax.axis_index("seq")
    me = lax.axis_index("head")
    size = min(256, rows)
    count = rows // size
    channels = heads * WIDTH * head_count

    spans = [pl.ds(b * size, size) for b in range(count)]
    blocks = range(count)

    def halves(x):
        return x[:, :WIDTH] + x[:, WIDTH:]

    def cols(h):
        return pl.ds(pl.multiple_of(h * WIDTH, WIDTH), WIDTH)

    def load(n, h):
        hbm, ref = ((k_hbm, k), (v_hbm, v), (q_hbm, q), (g_hbm, g))[n]
        return pltpu.make_async_copy(hbm.at[:, cols(h)], ref.at[:, cols(h)], in_sem.at[n, h])

    def store(n, h):
        hbm, ref = ((out_hbm, out), (dq_hbm, dq), (dk_hbm, dk), (dv_hbm, dv))[n]
        return pltpu.make_async_copy(ref.at[:, cols(h)], hbm.at[:, cols(h)], out_sem.at[n, h])

    def forward(h):
        return pltpu.make_async_remote_copy(
            src_ref=f_out.at[h], dst_ref=f_in.at[h], send_sem=f_send.at[h], recv_sem=f_recv.at[h],
            device_id=(lax.rem(z + 1, seq_count), me), device_id_type=MESH)

    def backward(h):
        return pltpu.make_async_remote_copy(
            src_ref=b_out.at[h], dst_ref=b_in.at[h], send_sem=b_send.at[h], recv_sem=b_recv.at[h],
            device_id=(lax.rem(z + seq_count - 1, seq_count), me), device_id_type=MESH)

    for h in range(heads):
        load(0, h).start()
        load(1, h).start()
    for h in range(heads):
        load(2, h).start()
        load(3, h).start()

    barrier = pltpu.get_barrier_semaphore()
    for step in range(1, head_count):
        pl.semaphore_signal(barrier, inc=1, device_id=(z, lax.rem(me + step, head_count)), device_id_type=MESH)
    for step in range(1, seq_count):
        pl.semaphore_signal(barrier, inc=1, device_id=(lax.rem(z + step, seq_count), me), device_id_type=MESH)

    below = lax.broadcasted_iota(jnp.int32, (size, size), 0) >= lax.broadcasted_iota(jnp.int32, (size, size), 1)
    above = lax.broadcasted_iota(jnp.int32, (size, size), 0) <= lax.broadcasted_iota(jnp.int32, (size, size), 1)
    tri = jnp.where(above, 1.0, 0.0).astype(f32)
    for b in range(count):
        at = pl.ds(b * size, size)
        along = jnp.dot(decay[:, at], tri, precision=highest, preferred_element_type=f32)
        for h in range(heads):
            sums_g[h, :, at] = along[h:h + 1]
    acc_sq[...] = jnp.zeros_like(acc_sq)
    acc_pr[...] = jnp.zeros_like(acc_pr)
    pl.semaphore_wait(barrier, head_count - 1 + seq_count - 1)

    def factor(h, b):
        return cols_g[(b + 1) * size - 1:(b + 1) * size, cols(h)]

    def states(h, carry):
        load(0, h).wait()
        load(1, h).wait()
        values = [v[at, cols(h)].astype(f32) for at in spans]
        key_blocks = [k[at, cols(h)] for at in spans]
        columns = [jnp.broadcast_to(sums_g[h, :, at], (WIDTH, size)).T for at in spans]
        lasts = [column[size - 1:size, :] for column in columns]
        to_ends = [jnp.exp(lasts[b] - columns[b]) for b in blocks]
        sides = [jnp.concatenate(split(values[b] * to_ends[b]), axis=1) for b in blocks]
        mine = [halves(dot(key_blocks[b], sides[b], 0, 0)) for b in blocks]
        state = jnp.zeros((WIDTH, WIDTH), f32)
        for b in blocks:
            state = jnp.exp(lasts[b]) * state + mine[b]
        for b in blocks:
            cols_g[spans[b], cols(h)] = columns[b]
            ends[spans[b], cols(h)] = to_ends[b]
            own[h, b] = mine[b]
        f_out[h] = state
        whole = jnp.exp(lasts[0])
        for b in range(1, count):
            whole = whole * jnp.exp(lasts[b])
        decays[h] = whole

        @pl.when(z == 0)
        def _():
            f_in[h] = jnp.zeros((WIDTH, WIDTH), f32)
            forward(h).start()
        return carry

    lax.fori_loop(0, heads, states, 0)

    def device_factor(h):
        return decays[h]

    def attend(h):
        load(2, h).wait()
        load(3, h).wait()
        columns = [cols_g[at, cols(h)] for at in spans]
        across = [sums_g[h, :, at] for at in spans]
        query_blocks = [q[at, cols(h)] for at in spans]
        key_blocks = [k[at, cols(h)] for at in spans]
        value_blocks = [v[at, cols(h)] for at in spans]
        scores = [dot(query_blocks[b], key_blocks[b], 1, 1) for b in blocks]
        masks = [
            jnp.exp(jnp.where(below, jnp.concatenate([columns[b]] * (size // WIDTH), axis=1) - across[b], -1e30))
            for b in blocks
        ]
        parts = [split(scores[b] * masks[b]) for b in blocks]
        inside = [dot(parts[b][0], value_blocks[b]) + dot(parts[b][1], value_blocks[b]) for b in blocks]
        for b in blocks:
            at = spans[b]
            mask[h, at, :] = masks[b]
            p_high[h, at, :] = parts[b][0].T
            p_low[h, at, :] = parts[b][1].T
            attn[at, cols(h)] = inside[b]
            cols_g[at, cols(h)] = jnp.exp(columns[b])

    def pass_forward(h):
        forward(h).wait_recv()
        f_out[h] = f_out[h] + device_factor(h) * f_in[h]
        forward(h).start()

    def enter(h, carry):
        @pl.when(z == seq_count - 1)
        def _():
            forward(h).wait_recv()

        state = f_in[h]
        factors = [factor(h, b) for b in blocks]
        own_blocks = [own[h, b] for b in blocks]
        query_blocks = [q[at, cols(h)] for at in spans]
        inside = [attn[at, cols(h)] for at in spans]
        starts = [cols_g[at, cols(h)] for at in spans]
        weights = [g[at, cols(h)].astype(f32) * gain[:, cols(h)] for at in spans]
        before = []
        for b in blocks:
            before.append(state)
            state = factors[b] * state + own_blocks[b]
        crosses = [
            dot(jnp.concatenate([query_blocks[b]] * 2, axis=1), jnp.concatenate(split(before[b]), axis=0))
            for b in blocks
        ]
        results = [inside[b] + starts[b] * crosses[b] for b in blocks]
        for b in blocks:
            at = spans[b]
            entering[h, b] = before[b]
            attn[at, cols(h)] = results[b]
            acc_sq[at, :] = acc_sq[at, :] + results[b] * results[b]
            acc_pr[at, :] = acc_pr[at, :] + results[b] * weights[b]

        return carry

    between = jnp.logical_and(z > 0, z < seq_count - 1)
    lag = jnp.where(between, jnp.minimum(heads, z - 1), 0)

    def forward_step(i, carry):
        @pl.when(jnp.logical_and(between, i >= lag))
        def _():
            pass_forward(i - lag)

        @pl.when(i < heads)
        def _():
            attend(i)
        return carry

    lax.fori_loop(0, heads + lag, forward_step, 0)
    lax.fori_loop(0, heads, enter, 0)

    for b in range(rows // WIDTH):
        at = pl.ds(b * WIDTH, WIDTH)
        norm[me, 0:1, at] = jnp.sum(acc_sq[at, :].T, axis=0, keepdims=True)
        norm[me, 1:2, at] = jnp.sum(acc_pr[at, :].T, axis=0, keepdims=True)

    def exchange(step):
        return pltpu.make_async_remote_copy(
            src_ref=norm.at[me], dst_ref=norm.at[me], send_sem=n_send.at[step], recv_sem=n_recv.at[step],
            device_id=(z, lax.rem(me + step, head_count)), device_id_type=MESH)

    def arrived(step):
        slot = norm.at[lax.rem(me + head_count - step, head_count)]
        return pltpu.make_async_remote_copy(
            src_ref=slot, dst_ref=slot, send_sem=n_send.at[step], recv_sem=n_recv.at[step],
            device_id=(z, lax.rem(me + step, head_count)), device_id_type=MESH)

    for step in range(1, head_count):
        exchange(step).start()
    for step in range(1, head_count):
        arrived(step).wait_recv()
    summed = norm[0]
    for d in range(1, head_count):
        summed = summed + norm[d]
    inverse = 1.0 / jnp.sqrt(summed[0:1] / channels + epsilon)
    second = inverse * inverse * inverse * (summed[1:2] / channels)
    for b in range(rows // WIDTH):
        at = slice(b * WIDTH, (b + 1) * WIDTH)
        alpha[at, :] = jnp.broadcast_to(inverse[:, at], (WIDTH, WIDTH)).T
        beta[at, :] = jnp.broadcast_to(second[:, at], (WIDTH, WIDTH)).T

    def gradients(h, carry):
        gain_h = gain[:, cols(h)]
        part = jnp.zeros((1, WIDTH), f32)
        state = jnp.zeros((WIDTH, WIDTH), f32)
        factors = [factor(h, b) for b in blocks]
        scales = [alpha[at, :] for at in spans]
        seconds = [beta[at, :] for at in spans]
        attended = [attn[at, cols(h)] for at in spans]
        cotangents = [g[at, cols(h)].astype(f32) for at in spans]
        starts = [cols_g[at, cols(h)] for at in spans]
        query_blocks = [q[at, cols(h)] for at in spans]
        grads = [
            scales[b] * (cotangents[b] * gain_h) - seconds[b] * attended[b] for b in blocks
        ]
        sides = [jnp.concatenate(split(grads[b] * starts[b]), axis=1) for b in blocks]
        mine = [halves(dot(query_blocks[b], sides[b], 0, 0)) for b in blocks]
        normed = [attended[b] * scales[b] for b in blocks]
        for b in reversed(blocks):
            part = part + jnp.sum(cotangents[b] * normed[b], axis=0, keepdims=True)
            state = factors[b] * state + mine[b]
        for b in blocks:
            at = spans[b]
            out[at, cols(h)] = (normed[b] * gain_h).astype(bf16)
            attn[at, cols(h)] = grads[b]
            back[h, b] = mine[b]
        gparts[z, :, cols(h)] = part
        b_out[h] = state
        store(0, h).start()

        @pl.when(z == seq_count - 1)
        def _():
            b_in[h] = jnp.zeros((WIDTH, WIDTH), f32)
            backward(h).start()
        return carry

    lax.fori_loop(0, heads, gradients, 0)

    def gain_copy(step, slot):
        return pltpu.make_async_remote_copy(
            src_ref=gparts.at[slot], dst_ref=gparts.at[slot], send_sem=g_send.at[step], recv_sem=g_recv.at[step],
            device_id=(lax.rem(z + step, seq_count), me), device_id_type=MESH)

    for step in range(1, seq_count):
        gain_copy(step, z).start()

    def relay(h):
        backward(h).wait_recv()
        b_out[h] = b_out[h] + device_factor(h) * b_in[h]
        backward(h).start()

    def inside_gradients(h):
        query_blocks = [q[at, cols(h)] for at in spans]
        key_blocks = [k[at, cols(h)] for at in spans]
        value_blocks = [v[at, cols(h)] for at in spans]
        parts = [split(attn[at, cols(h)]) for at in spans]
        masks = [mask[h, at, :] for at in spans]
        starts = [cols_g[at, cols(h)] for at in spans]
        states_in = [split(entering[h, b]) for b in blocks]
        highs = [p_high[h, at, :] for at in spans]
        lows = [p_low[h, at, :] for at in spans]
        both = [jnp.concatenate(parts[b], axis=1) for b in blocks]
        score_grads = [
            split(dot(both[b], jnp.concatenate([value_blocks[b]] * 2, axis=1), 1, 1) * masks[b]) for b in blocks
        ]
        crosses = [
            dot(both[b], jnp.concatenate([states_in[b][0]] * 2, axis=1), 1, 1)
            + dot(parts[b][0], states_in[b][1], 1, 1)
            for b in blocks
        ]
        value_parts = [halves(dot(highs[b], both[b])) + dot(lows[b], parts[b][0]) for b in blocks]
        query_parts = [
            dot(score_grads[b][0], key_blocks[b]) + dot(score_grads[b][1], key_blocks[b]) + starts[b] * crosses[b]
            for b in blocks
        ]
        key_parts = [
            dot(score_grads[b][0], query_blocks[b], 0, 0) + dot(score_grads[b][1], query_blocks[b], 0, 0)
            for b in blocks
        ]
        for b in blocks:
            at = spans[b]
            dq[at, cols(h)] = query_parts[b].astype(bf16)
            mask[h, at, 0:WIDTH] = key_parts[b]
            attn[at, cols(h)] = value_parts[b]
        store(1, h).start()

    def leave(h, carry):
        @pl.when(z == 0)
        def _():
            backward(h).wait_recv()

        state = b_in[h]
        factors = [factor(h, b) for b in blocks]
        back_blocks = [back[h, b] for b in blocks]
        key_blocks = [k[at, cols(h)] for at in spans]
        value_blocks = [v[at, cols(h)] for at in spans]
        to_ends = [ends[at, cols(h)] for at in spans]
        key_parts = [mask[h, at, 0:WIDTH] for at in spans]
        value_parts = [attn[at, cols(h)] for at in spans]
        after = [None] * count
        for b in reversed(blocks):
            after[b] = split(state)
            state = factors[b] * state + back_blocks[b]
        from_values = [
            dot(jnp.concatenate([value_blocks[b]] * 2, axis=1), jnp.concatenate(after[b], axis=1), 1, 1) for b in blocks
        ]
        from_keys = [
            dot(jnp.concatenate([key_blocks[b]] * 2, axis=1), jnp.concatenate(after[b], axis=0)) for b in blocks
        ]
        for b in blocks:
            at = spans[b]
            dk[at, cols(h)] = (key_parts[b] + to_ends[b] * from_values[b]).astype(bf16)
            dv[at, cols(h)] = (value_parts[b] + to_ends[b] * from_keys[b]).astype(bf16)
        store(2, h).start()
        store(3, h).start()
        return carry

    late = jnp.where(between, jnp.minimum(heads, 1 + 3 * (seq_count - 2 - z)), 0)

    def backward_step(i, carry):
        for r in range(2):
            j = 2 * (i - late) + r

            @pl.when(jnp.logical_and(between, jnp.logical_and(j >= 0, j < heads)))
            def _():
                relay(j)

        @pl.when(i < heads)
        def _():
            inside_gradients(i)
        return carry

    lax.fori_loop(0, heads + late, backward_step, 0)
    lax.fori_loop(0, heads, leave, 0)

    for step in range(1, seq_count):
        gain_copy(step, lax.rem(z + seq_count - step, seq_count)).wait_recv()
    result = gparts[0]
    for d in range(1, seq_count):
        result = result + gparts[d]
    dgain[...] = result

    for step in range(1, seq_count):
        gain_copy(step, z).wait_send()
    for step in range(1, head_count):
        exchange(step).wait_send()
    for h in range(heads):
        for n in range(4):
            store(n, h).wait()

    @pl.when(z < seq_count - 1)
    def _():
        for h in range(heads):
            forward(h).wait_send()

    @pl.when(z > 0)
    def _():
        for h in range(heads):
            backward(h).wait_send()


def hand_on(rows, *refs):
    sources, targets, held, in_sem, out_sem = refs[:5], refs[5:10], refs[10:14], refs[14], refs[15]
    pieces = 8
    step = rows // pieces
    arriving, leaving = [], []
    for p in range(pieces):
        for n in range(4):
            at = pl.ds(p * step, step)
            arriving.append(pltpu.make_async_copy(sources[n].at[at], held[n].at[at], in_sem.at[n, p]))
            leaving.append(pltpu.make_async_copy(held[n].at[at], targets[n].at[at], out_sem.at[n, p]))
    for copy in arriving:
        copy.start()
    targets[4][...] = sources[4][...]
    for first, second in zip(arriving, leaving):
        first.wait()
        second.start()
    for copy in leaving:
        copy.wait()


def local(queries, keys, values, log_decay, gain, out_grad):
    rows, channels = queries.shape
    heads = log_decay.shape[0]
    seq_count, head_count = lax.axis_size("seq"), lax.axis_size("head")
    size = min(256, rows)
    count = rows // size
    any_spec = pl.BlockSpec(memory_space=pl.ANY)
    vmem_spec = pl.BlockSpec(memory_space=pltpu.VMEM)
    narrow = jax.ShapeDtypeStruct((rows, channels), bf16)
    state = pltpu.VMEM((heads, WIDTH, WIDTH), f32)
    block_states = pltpu.VMEM((heads, count, WIDTH, WIDTH), f32)
    dma = pltpu.SemaphoreType.DMA
    results = pl.pallas_call(
        functools.partial(kernel, seq_count, head_count, heads, rows),
        out_shape=(narrow,) * 4 + (jax.ShapeDtypeStruct((1, channels), f32),),
        in_specs=[vmem_spec, vmem_spec] + [any_spec] * 4,
        out_specs=(any_spec,) * 4 + (vmem_spec,),
        scratch_shapes=[pltpu.VMEM((rows, channels), bf16)] * 8
        + [
            pltpu.VMEM((rows, channels), f32),
            pltpu.VMEM((heads, 1, rows), f32),
            pltpu.VMEM((rows, channels), f32),
            pltpu.VMEM((rows, channels), f32),
            block_states, block_states, block_states,
            pltpu.VMEM((heads, rows, size), f32),
            pltpu.VMEM((heads, rows, size), bf16),
            pltpu.VMEM((heads, rows, size), bf16),
            pltpu.VMEM((heads, 1, WIDTH), f32),
            state, state, state, state,
            pltpu.VMEM((rows, WIDTH), f32),
            pltpu.VMEM((rows, WIDTH), f32),
            pltpu.VMEM((head_count, 2, rows), f32),
            pltpu.VMEM((rows, WIDTH), f32),
            pltpu.VMEM((rows, WIDTH), f32),
            pltpu.VMEM((seq_count, 1, channels), f32),
            dma((4, heads)), dma((4, heads)),
            dma((heads,)), dma((heads,)), dma((heads,)), dma((heads,)),
            dma((head_count,)), dma((head_count,)), dma((seq_count,)), dma((seq_count,)),
        ],
        compiler_params=pltpu.CompilerParams(
            collective_id=0, has_side_effects=True, vmem_limit_bytes=60 * 1024 * 1024
        ),
        name="lightning",
    )(log_decay, gain.reshape(1, channels), queries, keys, values, out_grad)
    results = pl.pallas_call(
        functools.partial(hand_on, rows),
        out_shape=(narrow,) * 4 + (jax.ShapeDtypeStruct((1, channels), f32),),
        in_specs=[any_spec] * 4 + [vmem_spec],
        out_specs=(any_spec,) * 4 + (vmem_spec,),
        scratch_shapes=[pltpu.VMEM((rows, channels), bf16)] * 4 + [dma((4, 8)), dma((4, 8))],
        compiler_params=pltpu.CompilerParams(vmem_limit_bytes=60 * 1024 * 1024),
        name="hand_on",
    )(*results)
    return results[:4] + (results[4].reshape(channels),)


def solution(mesh):
    in_specs = (
        P("seq", "head"),
        P("seq", "head"),
        P("seq", "head"),
        P("head", "seq"),
        P("head"),
        P("seq", "head"),
    )
    out_specs = (P("seq", "head"), P("seq", "head"), P("seq", "head"), P("seq", "head"), P("head"))
    return jax.shard_map(local, mesh=mesh, in_specs=in_specs, out_specs=out_specs, check_vma=False)
```

```python
import functools

import jax
import jax.numpy as jnp
from jax import lax
from jax.experimental import pallas as pl
from jax.experimental.pallas import tpu as pltpu
from jax.sharding import PartitionSpec as P

epsilon = 1e-06
highest = lax.Precision.HIGHEST
MESH = pl.DeviceIdType.MESH
WIDTH = 128
f32, bf16 = jnp.float32, jnp.bfloat16


def dot(a, b, ca=1, cb=0):
    return lax.dot_general(a, b, (((ca,), (cb,)), ((), ())), preferred_element_type=f32)


def split(x):
    high = x.astype(bf16)
    return high, (x - high.astype(f32)).astype(bf16)


def kernel(
    seq_count, head_count, heads, rows,
    decay, gain, q_hbm, k_hbm, v_hbm, g_hbm,
    out_hbm, dq_hbm, dk_hbm, dv_hbm, dgain,
    q, k, v, g, out, dq, dk, dv,
    attn, sums_g, cols_g, ends, own, entering, back, mask, p_high, p_low,
    decays, f_in, f_out, b_in, b_out, acc_sq, acc_pr, norm, alpha, beta, gparts,
    in_sem, out_sem, f_send, f_recv, b_send, b_recv, n_send, n_recv, g_send, g_recv,
):
    z = lax.axis_index("seq")
    me = lax.axis_index("head")
    size = min(128, rows)
    count = rows // size
    channels = heads * WIDTH * head_count

    spans = [pl.ds(b * size, size) for b in range(count)]
    blocks = range(count)

    def halves(x):
        return x[:, :WIDTH] + x[:, WIDTH:]

    def cols(h):
        return pl.ds(pl.multiple_of(h * WIDTH, WIDTH), WIDTH)

    def load(n, h):
        hbm, ref = ((k_hbm, k), (v_hbm, v), (q_hbm, q), (g_hbm, g))[n]
        return pltpu.make_async_copy(hbm.at[:, cols(h)], ref.at[:, cols(h)], in_sem.at[n, h])

    def store(n, h):
        hbm, ref = ((out_hbm, out), (dq_hbm, dq), (dk_hbm, dk), (dv_hbm, dv))[n]
        return pltpu.make_async_copy(ref.at[:, cols(h)], hbm.at[:, cols(h)], out_sem.at[n, h])

    def forward(h):
        return pltpu.make_async_remote_copy(
            src_ref=f_out.at[h], dst_ref=f_in.at[h], send_sem=f_send.at[h], recv_sem=f_recv.at[h],
            device_id=(lax.rem(z + 1, seq_count), me), device_id_type=MESH)

    def backward(h):
        return pltpu.make_async_remote_copy(
            src_ref=b_out.at[h], dst_ref=b_in.at[h], send_sem=b_send.at[h], recv_sem=b_recv.at[h],
            device_id=(lax.rem(z + seq_count - 1, seq_count), me), device_id_type=MESH)

    for h in range(heads):
        load(0, h).start()
        load(1, h).start()
    for h in range(heads):
        load(2, h).start()
        load(3, h).start()

    barrier = pltpu.get_barrier_semaphore()
    for step in range(1, head_count):
        pl.semaphore_signal(barrier, inc=1, device_id=(z, lax.rem(me + step, head_count)), device_id_type=MESH)
    for step in range(1, seq_count):
        pl.semaphore_signal(barrier, inc=1, device_id=(lax.rem(z + step, seq_count), me), device_id_type=MESH)

    below = lax.broadcasted_iota(jnp.int32, (size, size), 0) >= lax.broadcasted_iota(jnp.int32, (size, size), 1)
    above = lax.broadcasted_iota(jnp.int32, (size, size), 0) <= lax.broadcasted_iota(jnp.int32, (size, size), 1)
    tri = jnp.where(above, 1.0, 0.0).astype(f32)
    for b in range(count):
        at = pl.ds(b * size, size)
        along = jnp.dot(decay[:, at], tri, precision=highest, preferred_element_type=f32)
        for h in range(heads):
            sums_g[h, :, at] = along[h:h + 1]
    acc_sq[...] = jnp.zeros_like(acc_sq)
    acc_pr[...] = jnp.zeros_like(acc_pr)
    pl.semaphore_wait(barrier, head_count - 1 + seq_count - 1)

    def factor(h, b):
        return cols_g[(b + 1) * size - 1:(b + 1) * size, cols(h)]

    def states(h, carry):
        load(0, h).wait()
        load(1, h).wait()
        values = [v[at, cols(h)].astype(f32) for at in spans]
        key_blocks = [k[at, cols(h)] for at in spans]
        columns = [jnp.broadcast_to(sums_g[h, :, at], (WIDTH, size)).T for at in spans]
        lasts = [column[size - 1:size, :] for column in columns]
        to_ends = [jnp.exp(lasts[b] - columns[b]) for b in blocks]
        sides = [jnp.concatenate(split(values[b] * to_ends[b]), axis=1) for b in blocks]
        mine = [halves(dot(key_blocks[b], sides[b], 0, 0)) for b in blocks]
        state = jnp.zeros((WIDTH, WIDTH), f32)
        for b in blocks:
            state = jnp.exp(lasts[b]) * state + mine[b]
        for b in blocks:
            cols_g[spans[b], cols(h)] = columns[b]
            ends[spans[b], cols(h)] = to_ends[b]
            own[h, b] = mine[b]
        f_out[h] = state
        whole = jnp.exp(lasts[0])
        for b in range(1, count):
            whole = whole * jnp.exp(lasts[b])
        decays[h] = whole

        @pl.when(z == 0)
        def _():
            f_in[h] = jnp.zeros((WIDTH, WIDTH), f32)
            forward(h).start()
        return carry

    lax.fori_loop(0, heads, states, 0)

    def device_factor(h):
        return decays[h]

    def attend(h):
        load(2, h).wait()
        load(3, h).wait()
        columns = [cols_g[at, cols(h)] for at in spans]
        across = [sums_g[h, :, at] for at in spans]
        query_blocks = [q[at, cols(h)] for at in spans]
        key_blocks = [k[at, cols(h)] for at in spans]
        value_blocks = [v[at, cols(h)] for at in spans]
        scores = [dot(query_blocks[b], key_blocks[b], 1, 1) for b in blocks]
        masks = [
            jnp.exp(jnp.where(below, jnp.concatenate([columns[b]] * (size // WIDTH), axis=1) - across[b], -1e30))
            for b in blocks
        ]
        parts = [split(scores[b] * masks[b]) for b in blocks]
        inside = [
            dot(jnp.concatenate(parts[b], axis=1), jnp.concatenate([value_blocks[b]] * 2, axis=0)) for b in blocks
        ]
        for b in blocks:
            at = spans[b]
            mask[h, at, :] = masks[b]
            p_high[h, at, :] = parts[b][0].T
            p_low[h, at, :] = parts[b][1].T
            attn[at, cols(h)] = inside[b]
            cols_g[at, cols(h)] = jnp.exp(columns[b])

    def pass_forward(h):
        forward(h).wait_recv()
        f_out[h] = f_out[h] + device_factor(h) * f_in[h]
        forward(h).start()

    def enter(h, carry):
        @pl.when(z == seq_count - 1)
        def _():
            forward(h).wait_recv()

        state = f_in[h]
        factors = [factor(h, b) for b in blocks]
        own_blocks = [own[h, b] for b in blocks]
        query_blocks = [q[at, cols(h)] for at in spans]
        inside = [attn[at, cols(h)] for at in spans]
        starts = [cols_g[at, cols(h)] for at in spans]
        weights = [g[at, cols(h)].astype(f32) * gain[:, cols(h)] for at in spans]
        before = []
        for b in blocks:
            before.append(state)
            state = factors[b] * state + own_blocks[b]
        crosses = [
            dot(jnp.concatenate([query_blocks[b]] * 2, axis=1), jnp.concatenate(split(before[b]), axis=0))
            for b in blocks
        ]
        results = [inside[b] + starts[b] * crosses[b] for b in blocks]
        for b in blocks:
            at = spans[b]
            entering[h, b] = before[b]
            attn[at, cols(h)] = results[b]
            acc_sq[at, :] = acc_sq[at, :] + results[b] * results[b]
            acc_pr[at, :] = acc_pr[at, :] + results[b] * weights[b]

        return carry

    between = jnp.logical_and(z > 0, z < seq_count - 1)
    lag = jnp.where(between, jnp.minimum(heads, z - 1), 0)

    def forward_step(i, carry):
        @pl.when(jnp.logical_and(between, i >= lag))
        def _():
            pass_forward(i - lag)

        @pl.when(i < heads)
        def _():
            attend(i)
        return carry

    lax.fori_loop(0, heads + lag, forward_step, 0)
    lax.fori_loop(0, heads, enter, 0)

    for b in range(rows // WIDTH):
        at = pl.ds(b * WIDTH, WIDTH)
        norm[me, 0:1, at] = jnp.sum(acc_sq[at, :].T, axis=0, keepdims=True)
        norm[me, 1:2, at] = jnp.sum(acc_pr[at, :].T, axis=0, keepdims=True)

    def exchange(step):
        return pltpu.make_async_remote_copy(
            src_ref=norm.at[me], dst_ref=norm.at[me], send_sem=n_send.at[step], recv_sem=n_recv.at[step],
            device_id=(z, lax.rem(me + step, head_count)), device_id_type=MESH)

    def arrived(step):
        slot = norm.at[lax.rem(me + head_count - step, head_count)]
        return pltpu.make_async_remote_copy(
            src_ref=slot, dst_ref=slot, send_sem=n_send.at[step], recv_sem=n_recv.at[step],
            device_id=(z, lax.rem(me + step, head_count)), device_id_type=MESH)

    for step in range(1, head_count):
        exchange(step).start()
    for step in range(1, head_count):
        arrived(step).wait_recv()
    summed = norm[0]
    for d in range(1, head_count):
        summed = summed + norm[d]
    inverse = 1.0 / jnp.sqrt(summed[0:1] / channels + epsilon)
    second = inverse * inverse * inverse * (summed[1:2] / channels)
    for b in range(rows // WIDTH):
        at = slice(b * WIDTH, (b + 1) * WIDTH)
        alpha[at, :] = jnp.broadcast_to(inverse[:, at], (WIDTH, WIDTH)).T
        beta[at, :] = jnp.broadcast_to(second[:, at], (WIDTH, WIDTH)).T

    def gradients(h, carry):
        gain_h = gain[:, cols(h)]
        part = jnp.zeros((1, WIDTH), f32)
        state = jnp.zeros((WIDTH, WIDTH), f32)
        factors = [factor(h, b) for b in blocks]
        scales = [alpha[at, :] for at in spans]
        seconds = [beta[at, :] for at in spans]
        attended = [attn[at, cols(h)] for at in spans]
        cotangents = [g[at, cols(h)].astype(f32) for at in spans]
        starts = [cols_g[at, cols(h)] for at in spans]
        query_blocks = [q[at, cols(h)] for at in spans]
        grads = [
            scales[b] * (cotangents[b] * gain_h) - seconds[b] * attended[b] for b in blocks
        ]
        sides = [jnp.concatenate(split(grads[b] * starts[b]), axis=1) for b in blocks]
        mine = [halves(dot(query_blocks[b], sides[b], 0, 0)) for b in blocks]
        normed = [attended[b] * scales[b] for b in blocks]
        for b in reversed(blocks):
            part = part + jnp.sum(cotangents[b] * normed[b], axis=0, keepdims=True)
            state = factors[b] * state + mine[b]
        for b in blocks:
            at = spans[b]
            out[at, cols(h)] = (normed[b] * gain_h).astype(bf16)
            attn[at, cols(h)] = grads[b]
            back[h, b] = mine[b]
        gparts[z, :, cols(h)] = part
        b_out[h] = state
        store(0, h).start()

        @pl.when(z == seq_count - 1)
        def _():
            b_in[h] = jnp.zeros((WIDTH, WIDTH), f32)
            backward(h).start()
        return carry

    lax.fori_loop(0, heads, gradients, 0)

    def gain_copy(step, slot):
        return pltpu.make_async_remote_copy(
            src_ref=gparts.at[slot], dst_ref=gparts.at[slot], send_sem=g_send.at[step], recv_sem=g_recv.at[step],
            device_id=(lax.rem(z + step, seq_count), me), device_id_type=MESH)

    for step in range(1, seq_count):
        gain_copy(step, z).start()

    def relay(h):
        backward(h).wait_recv()
        b_out[h] = b_out[h] + device_factor(h) * b_in[h]
        backward(h).start()

    def inside_gradients(h):
        query_blocks = [q[at, cols(h)] for at in spans]
        key_blocks = [k[at, cols(h)] for at in spans]
        value_blocks = [v[at, cols(h)] for at in spans]
        parts = [split(attn[at, cols(h)]) for at in spans]
        masks = [mask[h, at, :] for at in spans]
        starts = [cols_g[at, cols(h)] for at in spans]
        states_in = [split(entering[h, b]) for b in blocks]
        highs = [p_high[h, at, :] for at in spans]
        lows = [p_low[h, at, :] for at in spans]
        both = [jnp.concatenate(parts[b], axis=1) for b in blocks]
        rights = [
            jnp.concatenate(
                [jnp.concatenate([value_blocks[b]] * 2, axis=1), jnp.concatenate([states_in[b][0]] * 2, axis=1)], axis=0
            )
            for b in blocks
        ]
        products = [dot(both[b], rights[b], 1, 1) for b in blocks]
        rest = [dot(parts[b][0], states_in[b][1], 1, 1) for b in blocks]
        score_grads = [split(products[b][:, :size] * masks[b]) for b in blocks]
        rights = [
            jnp.concatenate(
                [both[b], jnp.concatenate([parts[b][0], jnp.zeros_like(parts[b][0])], axis=1)], axis=0
            )
            for b in blocks
        ]
        value_parts = [halves(dot(jnp.concatenate([highs[b], lows[b]], axis=1), rights[b])) for b in blocks]
        query_parts = [
            dot(jnp.concatenate(score_grads[b], axis=1), jnp.concatenate([key_blocks[b]] * 2, axis=0))
            + starts[b] * (products[b][:, size:] + rest[b])
            for b in blocks
        ]
        key_parts = [
            dot(jnp.concatenate(score_grads[b], axis=0), jnp.concatenate([query_blocks[b]] * 2, axis=0), 0, 0)
            for b in blocks
        ]
        for b in blocks:
            at = spans[b]
            dq[at, cols(h)] = query_parts[b].astype(bf16)
            mask[h, at, 0:WIDTH] = key_parts[b]
            attn[at, cols(h)] = value_parts[b]
        store(1, h).start()

    def leave(h, carry):
        @pl.when(z == 0)
        def _():
            backward(h).wait_recv()

        state = b_in[h]
        factors = [factor(h, b) for b in blocks]
        back_blocks = [back[h, b] for b in blocks]
        key_blocks = [k[at, cols(h)] for at in spans]
        value_blocks = [v[at, cols(h)] for at in spans]
        to_ends = [ends[at, cols(h)] for at in spans]
        key_parts = [mask[h, at, 0:WIDTH] for at in spans]
        value_parts = [attn[at, cols(h)] for at in spans]
        after = [None] * count
        for b in reversed(blocks):
            after[b] = split(state)
            state = factors[b] * state + back_blocks[b]
        from_values = [
            dot(jnp.concatenate([value_blocks[b]] * 2, axis=1), jnp.concatenate(after[b], axis=1), 1, 1) for b in blocks
        ]
        from_keys = [
            dot(jnp.concatenate([key_blocks[b]] * 2, axis=1), jnp.concatenate(after[b], axis=0)) for b in blocks
        ]
        for b in blocks:
            at = spans[b]
            dk[at, cols(h)] = (key_parts[b] + to_ends[b] * from_values[b]).astype(bf16)
            dv[at, cols(h)] = (value_parts[b] + to_ends[b] * from_keys[b]).astype(bf16)
        store(2, h).start()
        store(3, h).start()
        return carry

    late = jnp.where(between, jnp.minimum(heads, 1 + 3 * (seq_count - 2 - z)), 0)

    def backward_step(i, carry):
        for r in range(2):
            j = 2 * (i - late) + r

            @pl.when(jnp.logical_and(between, jnp.logical_and(j >= 0, j < heads)))
            def _():
                relay(j)

        @pl.when(i < heads)
        def _():
            inside_gradients(i)
        return carry

    lax.fori_loop(0, heads + late, backward_step, 0)
    lax.fori_loop(0, heads, leave, 0)

    for step in range(1, seq_count):
        gain_copy(step, lax.rem(z + seq_count - step, seq_count)).wait_recv()
    result = gparts[0]
    for d in range(1, seq_count):
        result = result + gparts[d]
    dgain[...] = result

    for step in range(1, seq_count):
        gain_copy(step, z).wait_send()
    for step in range(1, head_count):
        exchange(step).wait_send()
    for h in range(heads):
        for n in range(4):
            store(n, h).wait()

    @pl.when(z < seq_count - 1)
    def _():
        for h in range(heads):
            forward(h).wait_send()

    @pl.when(z > 0)
    def _():
        for h in range(heads):
            backward(h).wait_send()


def hand_on(rows, *refs):
    sources, targets, held, in_sem, out_sem = refs[:5], refs[5:10], refs[10:14], refs[14], refs[15]
    pieces = 8
    step = rows // pieces
    arriving, leaving = [], []
    for p in range(pieces):
        for n in range(4):
            at = pl.ds(p * step, step)
            arriving.append(pltpu.make_async_copy(sources[n].at[at], held[n].at[at], in_sem.at[n, p]))
            leaving.append(pltpu.make_async_copy(held[n].at[at], targets[n].at[at], out_sem.at[n, p]))
    for copy in arriving:
        copy.start()
    targets[4][...] = sources[4][...]
    for first, second in zip(arriving, leaving):
        first.wait()
        second.start()
    for copy in leaving:
        copy.wait()


def local(queries, keys, values, log_decay, gain, out_grad):
    rows, channels = queries.shape
    heads = log_decay.shape[0]
    seq_count, head_count = lax.axis_size("seq"), lax.axis_size("head")
    size = min(128, rows)
    count = rows // size
    any_spec = pl.BlockSpec(memory_space=pl.ANY)
    vmem_spec = pl.BlockSpec(memory_space=pltpu.VMEM)
    narrow = jax.ShapeDtypeStruct((rows, channels), bf16)
    state = pltpu.VMEM((heads, WIDTH, WIDTH), f32)
    block_states = pltpu.VMEM((heads, count, WIDTH, WIDTH), f32)
    dma = pltpu.SemaphoreType.DMA
    results = pl.pallas_call(
        functools.partial(kernel, seq_count, head_count, heads, rows),
        out_shape=(narrow,) * 4 + (jax.ShapeDtypeStruct((1, channels), f32),),
        in_specs=[vmem_spec, vmem_spec] + [any_spec] * 4,
        out_specs=(any_spec,) * 4 + (vmem_spec,),
        scratch_shapes=[pltpu.VMEM((rows, channels), bf16)] * 8
        + [
            pltpu.VMEM((rows, channels), f32),
            pltpu.VMEM((heads, 1, rows), f32),
            pltpu.VMEM((rows, channels), f32),
            pltpu.VMEM((rows, channels), f32),
            block_states, block_states, block_states,
            pltpu.VMEM((heads, rows, size), f32),
            pltpu.VMEM((heads, rows, size), bf16),
            pltpu.VMEM((heads, rows, size), bf16),
            pltpu.VMEM((heads, 1, WIDTH), f32),
            state, state, state, state,
            pltpu.VMEM((rows, WIDTH), f32),
            pltpu.VMEM((rows, WIDTH), f32),
            pltpu.VMEM((head_count, 2, rows), f32),
            pltpu.VMEM((rows, WIDTH), f32),
            pltpu.VMEM((rows, WIDTH), f32),
            pltpu.VMEM((seq_count, 1, channels), f32),
            dma((4, heads)), dma((4, heads)),
            dma((heads,)), dma((heads,)), dma((heads,)), dma((heads,)),
            dma((head_count,)), dma((head_count,)), dma((seq_count,)), dma((seq_count,)),
        ],
        compiler_params=pltpu.CompilerParams(
            collective_id=0, has_side_effects=True, vmem_limit_bytes=60 * 1024 * 1024
        ),
        name="lightning",
    )(log_decay, gain.reshape(1, channels), queries, keys, values, out_grad)
    results = pl.pallas_call(
        functools.partial(hand_on, rows),
        out_shape=(narrow,) * 4 + (jax.ShapeDtypeStruct((1, channels), f32),),
        in_specs=[any_spec] * 4 + [vmem_spec],
        out_specs=(any_spec,) * 4 + (vmem_spec,),
        scratch_shapes=[pltpu.VMEM((rows, channels), bf16)] * 4 + [dma((4, 8)), dma((4, 8))],
        compiler_params=pltpu.CompilerParams(vmem_limit_bytes=60 * 1024 * 1024),
        name="hand_on",
    )(*results)
    return results[:4] + (results[4].reshape(channels),)


def solution(mesh):
    in_specs = (
        P("seq", "head"),
        P("seq", "head"),
        P("seq", "head"),
        P("head", "seq"),
        P("head"),
        P("seq", "head"),
    )
    out_specs = (P("seq", "head"), P("seq", "head"), P("seq", "head"), P("seq", "head"), P("head"))
    return jax.shard_map(local, mesh=mesh, in_specs=in_specs, out_specs=out_specs, check_vma=False)
```
